128 devices in a mesh: rep: 8 (over y, core), shard: 16 (over x, z).
Axes of the slice: x: 4, y: 4, z: 4, core: 2. Of those that a mesh axis runs over, the one named last changes fastest.
Arguments:
- tokens: bfloat16 [16384, 1024], P(('rep', 'shard')), may hold values from -6 to 6
- doc_ids: int32 [16384], P(('rep', 'shard')), may hold values from -1 to 2, as said below
- grad_out: bfloat16 [16384, 1024], P(('rep', 'shard')), may hold values from -6 to 6
- norm_gains: bfloat16 [2, 2, 1024], P(None, None, 'shard'), may hold values from 0.25 to 1.75
- shifts: bfloat16 [2, 4, 1024], P(None, None, 'shard'), may hold values from -2 to 2
- qkv_weight: bfloat16 [2, 1024, 3072], P(None, 'shard'), may hold values from -0.1875 to 0.1875
- qkv_bias: bfloat16 [2, 3072], P(None, 'shard'), may hold values from -2 to 2
- dense_weight: bfloat16 [2, 1024, 1024], P(None, 'shard'), may hold values from -0.5 to 0.5
- up_weight: bfloat16 [2, 1024, 4096], P(None, 'shard'), may hold values from -0.1875 to 0.1875
- up_bias: bfloat16 [2, 4096], P(None, 'shard'), may hold values from -2 to 2
- down_weight: bfloat16 [2, 4096, 1024], P(None, 'shard'), may hold values from -0.09375 to 0.09375
Outputs:
- output: bfloat16 [16384, 1024], P(('rep', 'shard'))
- input_grad: float32 [16384, 1024], P(('rep', 'shard'))
- grad_norm_gains: float32 [2, 2, 1024], P(None, None, 'shard')
- grad_shifts: float32 [2, 4, 1024], P(None, None, 'shard')
- grad_qkv_weight: float32 [2, 1024, 3072], P(None, 'shard')
- grad_qkv_bias: float32 [2, 3072], P(None, 'shard')
- grad_dense_weight: float32 [2, 1024, 1024], P(None, 'shard')
- grad_up_weight: float32 [2, 1024, 4096], P(None, 'shard')
- grad_up_bias: float32 [2, 4096], P(None, 'shard')
- grad_down_weight: float32 [2, 4096, 1024], P(None, 'shard')
The draws below stay inside these ranges and needn't reach their ends.
Inputs may be any that keep to these rules, and one draw needn't show every extreme that they name: `doc_ids`: within each aligned block of 128 slots (one device's), the ids start at 0 in the first slot, never fall, and are followed by -1 in the unused slots; at least half of a block's slots are used, and in some block all are.
All inputs are finite; a program needn't handle non-finite values.
Results may differ from the reference program's by a relative error of at most 0.02.
Values may be sent and summed in bfloat16 or wider, within the bound.
No kernel may reach another device: no remote copies, remote signals or barrier semaphores. Data moves between devices by JAX's collectives and lax.ppermute only.
A program may use at most 192 MiB of HBM per device.

```python
import math
import jax
import jax.numpy as jnp
from jax import lax

D = 1024
HEADS = 16
HEAD_DIM = 64
FF = 4096
ROT = 16
LAYERS = 2
TOK_DEV = 128
TOKENS = 16384


def draw_doc_ids(key, part):
    key = jax.random.fold_in(key, 11)
    blocks = TOKENS // TOK_DEV
    key_live, key_cut, key_full = jax.random.split(key, 3)
    live_count = jax.random.randint(key_live, (blocks,), TOK_DEV // 2, TOK_DEV + 1)
    full_block = jax.random.randint(key_full, (), 0, blocks)
    live_count = jnp.where(jnp.arange(blocks) == full_block, TOK_DEV, live_count)
    cut_points = jax.random.randint(key_cut, (blocks, 2), 1, TOK_DEV)
    slot_ids = jnp.arange(TOK_DEV)[None, :]
    doc_values = (slot_ids >= cut_points[:, :1]).astype(jnp.int32) + (slot_ids >= cut_points[:, 1:]).astype(jnp.int32)
    doc_values = jnp.where(slot_ids < live_count[:, None], doc_values, -1)
    return doc_values.reshape(TOKENS).astype(jnp.int32)


def block_levels(key, extent, pieces, low, high):
    def one(axis_at, parts):
        steps = jax.random.uniform(jax.random.fold_in(jax.random.fold_in(key, 6), axis_at), (parts,), jnp.float32, low / len(pieces), high / len(pieces))
        return jnp.repeat(jnp.exp(steps), extent[axis_at] // parts).reshape((-1,) + (1,) * (len(extent) - axis_at - 1))

    loudness = one(*pieces[0])
    for cut in pieces[1:]:
        loudness = loudness * one(*cut)
    return loudness


def gaussian(own_key, dims, scale, limit, pieces=(), kind=jnp.bfloat16):
    level = block_levels(own_key, dims, pieces, -0.22, 0.18) if pieces else 1.0
    values = jax.random.normal(own_key, dims, jnp.float32) * scale * level
    return jnp.minimum(jnp.maximum(values, -limit), limit).astype(kind)


def setup_inputs(seed: int = 0) -> dict:
    streams_of = jax.random.split(jax.random.key(seed), 12)
    tokens = gaussian(streams_of[0], (TOKENS, D), 1.0, 6.0, ((0, 128),))
    doc_ids = draw_doc_ids(jax.random.fold_in(streams_of[11], 71), 0)
    grad_out = gaussian(streams_of[2], (TOKENS, D), 1.0, 6.0, ((0, 128),))
    norm_gains = jnp.clip(1.0 + 0.15 * jax.random.normal(streams_of[3], (LAYERS, 2, D), jnp.float32), 0.25, 1.75).astype(jnp.bfloat16)
    shifts = gaussian(streams_of[4], (LAYERS, 4, D), 0.3, 2.0, ((2, 16),))
    qkv_weight = gaussian(streams_of[5], (LAYERS, D, 3 * D), D ** -0.5, 0.1875, ((1, 16),))
    qkv_bias = gaussian(streams_of[6], (LAYERS, 3 * D), 0.3, 2.0, ((1, 16),))
    dense_weight = gaussian(streams_of[7], (LAYERS, D, D), (D // 8) ** -0.5, 0.5, ((1, 16),))
    up_weight = gaussian(streams_of[8], (LAYERS, D, FF), D ** -0.5, 0.1875, ((1, 16),))
    up_bias = gaussian(streams_of[9], (LAYERS, FF), 0.3, 2.0, ((1, 16),))
    down_weight = gaussian(streams_of[10], (LAYERS, FF, D), FF ** -0.5, 0.09375, ((1, 16),))
    return dict(tokens=tokens, doc_ids=doc_ids, grad_out=grad_out, norm_gains=norm_gains, shifts=shifts, qkv_weight=qkv_weight, qkv_bias=qkv_bias, dense_weight=dense_weight, up_weight=up_weight, up_bias=up_bias, down_weight=down_weight)


epsilon = 1e-05
highest = lax.Precision.HIGHEST

@jax.custom_vjp
def low(v):
    return lax.optimization_barrier(v.astype(jnp.bfloat16)).astype(jnp.float32)

@jax.custom_vjp
def low_back(v):
    return v

def low_keep(v):
    return (low(v), None)

def low_pass(kept, grad):
    return (grad,)

def back_keep(v):
    return (v, None)

def back_low(kept, grad):
    return (low(grad),)
low.defvjp(low_keep, low_pass)
low_back.defvjp(back_keep, back_low)

def norm_rows(values, gain_row, shift_row):
    average = lax.optimization_barrier(jnp.mean(values, axis=-1, keepdims=True))
    centered = values - average
    spread = lax.optimization_barrier(jnp.mean(centered * centered, axis=-1, keepdims=True))
    return centered * lax.rsqrt(spread + epsilon) * gain_row + shift_row

def gelu_exact(values):
    return jax.nn.gelu(values, approximate=False)

def rotary_tables(doc_block):
    rows_here = doc_block.shape[0]
    slot_ids = jnp.arange(rows_here)
    same_doc = (doc_block[None, :] == doc_block[:, None]) & (slot_ids[None, :] < slot_ids[:, None])
    places = lax.optimization_barrier(jnp.sum(same_doc.astype(jnp.float32), axis=1))
    half_rot = ROT // 2
    frequency = jnp.exp(jnp.arange(half_rot, dtype=jnp.float32) * (-2.0 * math.log(10000.0) / ROT))
    angles = places[:, None] * frequency[None, :]
    return (jnp.cos(angles)[:, None, :], jnp.sin(angles)[:, None, :])

def rotate(values, cosine, sine_rot):
    half_rot = ROT // 2
    first_part = values[..., :half_rot]
    second_part = values[..., half_rot:ROT]
    rest_part = values[..., ROT:]
    return jnp.concatenate([first_part * cosine - second_part * sine_rot, second_part * cosine + first_part * sine_rot, rest_part], axis=-1)

def attend_block(block_in):
    queries, keys_r, values_v, doc_block = block_in
    rows_here = doc_block.shape[0]
    slot_ids = jnp.arange(rows_here)
    allowed = (doc_block[None, :] == doc_block[:, None]) & (slot_ids[None, :] <= slot_ids[:, None])
    scores = low_back(jnp.einsum('qhd,khd->hqk', queries, keys_r, precision=highest) * HEAD_DIM ** (-0.5))
    scores = jnp.where(allowed[None], scores, -1e+30)
    row_max = lax.optimization_barrier(jnp.max(scores, axis=-1, keepdims=True))
    weights_e = jnp.exp(scores - row_max)
    probs = low(weights_e / lax.optimization_barrier(jnp.sum(weights_e, axis=-1, keepdims=True)))
    return jnp.einsum('hqk,khd->qhd', probs, values_v, precision=highest)

def layer_forward(current, weights, cosine, sine_rot, doc_blocks):
    w_qkv, w_dense, w_up, w_down, gain_rows, shift_rows, b_qkv, b_up = weights
    rows_here = current.shape[0]
    features = current.shape[1]
    blocks = rows_here // TOK_DEV
    first_in = low(norm_rows(current, gain_rows[0], shift_rows[0]))
    mixed_qkv = low_back(jnp.dot(first_in, w_qkv, precision=highest) + b_qkv)
    queries = low(rotate(mixed_qkv[:, :features].reshape(rows_here, HEADS, HEAD_DIM), cosine, sine_rot))
    keys_r = low(rotate(mixed_qkv[:, features:2 * features].reshape(rows_here, HEADS, HEAD_DIM), cosine, sine_rot))
    values_v = low(mixed_qkv[:, 2 * features:].reshape(rows_here, HEADS, HEAD_DIM))
    attended = lax.map(jax.checkpoint(attend_block), (queries.reshape(blocks, TOK_DEV, HEADS, HEAD_DIM), keys_r.reshape(blocks, TOK_DEV, HEADS, HEAD_DIM), values_v.reshape(blocks, TOK_DEV, HEADS, HEAD_DIM), doc_blocks))
    attn_flat = low_back(low(attended.reshape(rows_here, features)))
    branch_a = low_back(jnp.dot(attn_flat, w_dense, precision=highest) + shift_rows[2])
    second_in = low(norm_rows(current, gain_rows[1], shift_rows[1]))
    up_pre = low_back(jnp.dot(second_in, w_up, precision=highest) + b_up)
    activated = low(gelu_exact(up_pre))
    branch_m = low_back(jnp.dot(activated, w_down, precision=highest) + shift_rows[3])
    return current + branch_a + branch_m

def reference(tokens, doc_ids, grad_out, norm_gains, shifts, qkv_weight, qkv_bias, dense_weight, up_weight, up_bias, down_weight):
    blocks = TOKENS // TOK_DEV
    doc_blocks = doc_ids.reshape(blocks, TOK_DEV)
    cosine, sine_rot = lax.map(rotary_tables, doc_blocks)
    cosine = cosine.reshape(TOKENS, 1, ROT // 2)
    sine_rot = sine_rot.reshape(TOKENS, 1, ROT // 2)
    params = (qkv_weight.astype(jnp.float32), dense_weight.astype(jnp.float32), up_weight.astype(jnp.float32), down_weight.astype(jnp.float32), norm_gains.astype(jnp.float32), shifts.astype(jnp.float32), qkv_bias.astype(jnp.float32), up_bias.astype(jnp.float32))

    def forward(current, weights):
        for number in range(LAYERS):
            layer_weights = tuple((array_in[number] for array_in in weights))
            current = layer_forward(current, layer_weights, cosine, sine_rot, doc_blocks)
        return current
    result, pullback = jax.vjp(forward, tokens.astype(jnp.float32), params)
    live_rows = (doc_ids >= 0).astype(jnp.float32)[:, None]
    grad_input, grad_params = pullback(grad_out.astype(jnp.float32) * live_rows)
    return (result.astype(jnp.bfloat16), grad_input, grad_params[4], grad_params[5], grad_params[0], grad_params[6], grad_params[1], grad_params[2], grad_params[7], grad_params[3])
```

```python
import math

import jax
import jax.numpy as jnp
import numpy as np
from jax import lax
from jax.experimental import pallas as pl
from jax.experimental.pallas import tpu as pltpu
from jax.sharding import PartitionSpec as P

HEADS = 16
HEAD_DIM = 64
ROT = 16
LAYERS = 2
D = 1024
FF = 4096
TOK = 128
REPS = 8
SHARDS = 16
ROWS = REPS * TOK
QKV_R = 3 * D // REPS
FF_R = FF // REPS
A_LANES = QKV_R + FF_R
UNIT = FF // SHARDS // REPS
STEP = 256
EPS = 1e-05
VMEM_LIMIT = 48 * 2**20

BF = jnp.bfloat16
F32 = jnp.float32


def take_y(k):
    return [(((y + k) % 4) * 2 + c, y * 2 + c) for y in range(4) for c in range(2)]


CORE_FLIP = [(y * 2 + 1 - c, y * 2 + c) for y in range(4) for c in range(2)]


def fetch_y(a, k):
    return lax.ppermute(a, "rep", take_y(k % 4))


def flip_core(a):
    return lax.ppermute(a, "rep", CORE_FLIP)


Y_GROUPS = [[0, 2, 4, 6], [1, 3, 5, 7]]


def along_y(a):
    return lax.all_to_all(a, "rep", 0, 0, axis_index_groups=Y_GROUPS, tiled=True)


def gather_rep(block):
    near = [block] + [fetch_y(block, k) for k in (1, 2, 3)]
    return near + [flip_core(piece) for piece in near]


def gather_rep_ordered(block, y):
    near = jnp.zeros((4,) + block.shape, block.dtype)
    for k in range(4):
        piece = block if k == 0 else fetch_y(block, k)
        near = lax.dynamic_update_slice_in_dim(near, piece[None], (y + k) % 4, 0)
    return near, flip_core(near)


def gather_rep_at_once(block):
    near = along_y(jnp.broadcast_to(block[None], (4,) + block.shape))
    return near, flip_core(near)


def scatter_rep(near, far):
    near = near.reshape(4, TOK, D).astype(F32)
    far = flip_core(far).reshape(4, TOK, D).astype(F32)
    moved = [fetch_y((near[k] + far[k]).astype(BF), -k) for k in (1, 2, 3)]
    total = near[0] + far[0]
    for piece in moved:
        total = total + piece.astype(F32)
    return total


def gather_shard(a):
    return lax.all_to_all(jnp.broadcast_to(a[None], (SHARDS,) + a.shape), "shard", 0, 0, tiled=True)


def scatter_shard(a):
    return jnp.sum(lax.all_to_all(a, "shard", 0, 0, tiled=True).astype(F32), axis=0).astype(BF)


DENSE_IN = [((s // 2) * 16 + 2 * r + s % 2, r * 16 + s) for r in range(REPS) for s in range(SHARDS)]
SHARD_PAIR = [(s ^ 1, s) for s in range(SHARDS)]
DENSE_OUT = [((s // 2) * 16 + 8 * (s % 2) + r, r * 16 + s) for r in range(REPS) for s in range(SHARDS)]


def gather_dense(local, s):
    one = lax.ppermute(local, ("rep", "shard"), DENSE_IN)
    two = lax.ppermute(one, "shard", SHARD_PAIR)
    even = s % 2 == 0
    return jnp.concatenate([jnp.where(even, one, two), jnp.where(even, two, one)], axis=1)


def dot(a, b):
    return lax.dot_general(a, b, (((1,), (0,)), ((), ())), preferred_element_type=F32)


def dot_nt(a, b):
    return lax.dot_general(a, b, (((1,), (1,)), ((), ())), preferred_element_type=F32)


def dot_tn(a, b):
    return lax.dot_general(a, b, (((0,), (0,)), ((), ())), preferred_element_type=F32)


def params():
    return pltpu.CompilerParams(vmem_limit_bytes=VMEM_LIMIT)


VMEM = pl.BlockSpec(memory_space=pltpu.VMEM)
SMEM = pl.BlockSpec(memory_space=pltpu.SMEM)


def pack_kernel(place_ref, qkv_ref, up_ref, down_ref, slots_ref, a_ref, b_ref):
    r, s = place_ref[0], place_ref[1]
    lane = lax.broadcasted_iota(jnp.int32, (64, 128), 1)
    row = lax.broadcasted_iota(jnp.int32, (64, 128), 0)
    for layer in range(LAYERS):
        for part in range(3):
            start = pl.multiple_of(part * D + 128 * r, 128)
            a_ref[layer, :, part * 128 : (part + 1) * 128] = qkv_ref[layer, :, pl.ds(start, 128)]
        for group in range(4):
            merged = jnp.zeros((64, 128), F32)
            for sub in range(4):
                start = pl.multiple_of(256 * (4 * group + sub) + 128 * (r // 4), 128)
                piece = up_ref[layer, :, pl.ds(start, 128)].astype(F32)
                turned = pltpu.roll(piece, (32 * sub + 128 - 32 * (r % 4)) % 128, 1)
                merged = jnp.where(lane // 32 == sub, turned, merged)
            low = QKV_R + group * 128
            a_ref[layer, :, low : low + 128] = merged.astype(BF)
        b_ref[layer] = down_ref[layer, pl.ds(pl.multiple_of(UNIT * r, UNIT), UNIT), :]
        slots = slots_ref[layer]
        side = jnp.zeros((64, 128), F32)
        for vector, slot in enumerate((0, 2, 1, 3, 4, 5)):
            here = (row == 8 * vector + s // 2) & (lane // 64 == s % 2)
            side = jnp.where(here, slots[slot : slot + 1], side)
        for third in range(3):
            block = 3 * s + third
            target = jnp.where((block // 2) % 8 == r, 48 + block // 16, -1)
            here = (row == target) & (lane // 64 == block % 2)
            side = jnp.where(here, slots[6 + third : 7 + third], side)
        piece = jnp.where(r // 4 == 0, slots[9:10], slots[10:11])
        turned = pltpu.roll(jnp.broadcast_to(piece, (64, 128)), (32 * (s % 4) + 128 - 32 * (r % 4)) % 128, 1)
        side = jnp.where((row == 51 + s // 4) & (lane // 32 == s % 4), turned, side)
        a_ref[layer, :, A_LANES:] = side.astype(BF)


def pack(place, qkv_weight, up_weight, down_weight, slots):
    return pl.pallas_call(
        pack_kernel,
        in_specs=[SMEM, VMEM, VMEM, VMEM, VMEM],
        out_specs=[VMEM, VMEM],
        out_shape=[
            jax.ShapeDtypeStruct((LAYERS, 64, D), BF),
            jax.ShapeDtypeStruct((LAYERS, UNIT, D), BF),
        ],
        compiler_params=params(),
        name="pack",
    )(place, qkv_weight, up_weight, down_weight, slots)


def unpack_kernel(rep_ref, *refs):
    pieces, (qkv_ref, up_ref, down_ref, dense_ref) = refs[:8], refs[8:]
    c = rep_ref[0] % 2
    lane = lax.broadcasted_iota(jnp.int32, (64, 128), 1)
    for layer in range(LAYERS):
        a_near, a_far, b_near, b_far = pieces[4 * layer : 4 * layer + 4]
        whole = []
        for r in range(REPS):
            mine = c == r % 2
            piece = jnp.where(mine, a_near[r // 2], a_far[r // 2]).astype(F32)
            for part in range(3):
                low = part * D + 128 * r
                qkv_ref[layer, :, low : low + 128] = piece[:, part * 128 : (part + 1) * 128]
            whole.append(piece[:, QKV_R:A_LANES])
            piece = jnp.where(mine, b_near[r // 2], b_far[r // 2]).astype(F32)
            down_ref[layer, UNIT * r : UNIT * (r + 1), :] = piece[:UNIT]
            dense_ref[layer, 8 * r : 8 * r + 8, :] = piece[UNIT : UNIT + 8]
        for s in range(SHARDS):
            group, sub = s // 4, s % 4
            for half in range(2):
                merged = jnp.zeros((64, 128), F32)
                for inner in range(4):
                    piece = whole[4 * half + inner][:, group * 128 : (group + 1) * 128]
                    shift = (32 * inner - 32 * sub) % 128
                    turned = pltpu.roll(piece, shift, 1) if shift else piece
                    merged = jnp.where(lane // 32 == inner, turned, merged)
                low = 256 * s + 128 * half
                up_ref[layer, :, low : low + 128] = merged


def unpack(rep, *pieces):
    return pl.pallas_call(
        unpack_kernel,
        in_specs=[SMEM] + [VMEM] * 8,
        out_specs=[VMEM] * 4,
        out_shape=[
            jax.ShapeDtypeStruct((LAYERS, 64, 3 * D), F32),
            jax.ShapeDtypeStruct((LAYERS, 64, FF), F32),
            jax.ShapeDtypeStruct((LAYERS, 256, D), F32),
            jax.ShapeDtypeStruct((LAYERS, 64, D), F32),
        ],
        compiler_params=params(),
        name="unpack",
    )(rep, *pieces)


def turn(values, cos_t, low_t, high_t):
    return values * cos_t + pltpu.roll(values, 120, 1) * low_t + pltpu.roll(values, 8, 1) * high_t


def turn_back(values, cos_t, low_t, high_t):
    return values * cos_t - pltpu.roll(values, 120, 1) * low_t - pltpu.roll(values, 8, 1) * high_t


def row_spec(lanes):
    return pl.BlockSpec((STEP, lanes), lambda i: (i, 0))


def whole_spec(shape):
    return pl.BlockSpec(shape, lambda i: (0,) * len(shape))


PROB_SPEC = pl.BlockSpec((STEP // TOK, 2, TOK, TOK), lambda i: (i, 0, 0, 0))
WA_SPEC = whole_spec((D, D))
WD_SPEC = whole_spec((FF_R, D))
WO_SPEC = whole_spec((128, D))
VEC_SPEC = whole_spec((16, D))
NEAR_SPEC = pl.BlockSpec((STEP, D), lambda i: (jnp.minimum(i, 1), 0))
FAR_SPEC = pl.BlockSpec((STEP, D), lambda i: (jnp.maximum(i - 2, 0), 0))


def rows_of(lanes, dtype):
    return jax.ShapeDtypeStruct((ROWS, lanes), dtype)


def put_block(near_ref, far_ref, values):
    @pl.when(pl.program_id(0) < 2)
    def _():
        near_ref[...] = values

    @pl.when(pl.program_id(0) >= 2)
    def _():
        far_ref[...] = values


def inner_kernel(*refs):
    pieces, (wa_ref, mask_ref, cos_ref, low_ref, high_ref) = refs[:REPS], refs[REPS : REPS + 5]
    xh_ref, qkv_ref, prob_ref, o_ref, act_ref, slope_ref, vec_ref = refs[REPS + 5 :]

    @pl.when(pl.program_id(0) == 0)
    def _():
        side = jnp.zeros((64, 128), F32)
        for shard in range(SHARDS):
            side = side + wa_ref[64 * shard : 64 * (shard + 1), A_LANES:].astype(F32)
        vec_ref[...] = jnp.zeros_like(vec_ref)
        for vector in range(6):
            for j in range(8):
                vec_ref[vector : vector + 1, 128 * j : 128 * (j + 1)] = side[8 * vector + j : 8 * vector + j + 1]
        for j in range(7):
            vec_ref[6:7, 128 * j : 128 * (j + 1)] = side[48 + j : 49 + j]

    for step in range(4):

        @pl.when(pl.program_id(0) == step)
        def _(step=step):
            xh_ref[:TOK] = pieces[2 * step][...]
            xh_ref[TOK:] = pieces[2 * step + 1][...]

    xh = xh_ref[...].astype(F32)
    h1 = (xh * vec_ref[0:1] + vec_ref[1:2]).astype(BF)
    h2 = (xh * vec_ref[2:3] + vec_ref[3:4]).astype(BF)
    mixed = dot(h1, wa_ref[:, :QKV_R]) + vec_ref[6:7, :QKV_R]
    tables = (cos_ref[...], low_ref[...], high_ref[...])
    q = turn(mixed[:, :128], *tables).astype(BF)
    k = turn(mixed[:, 128:256], *tables).astype(BF)
    v = mixed[:, 256:].astype(BF)
    qkv_ref[:, :128] = q
    qkv_ref[:, 128:256] = k
    qkv_ref[:, 256:] = v
    u = dot(h2, wa_ref[:, QKV_R:A_LANES]) + vec_ref[6:7, QKV_R:A_LANES]
    share = 0.5 * (1.0 + lax.erf(u * math.sqrt(0.5)))
    act_ref[...] = (u * share).astype(BF)
    slope_ref[...] = share + u * jnp.exp(-0.5 * u * u) * (1.0 / math.sqrt(2.0 * math.pi))
    first = lax.broadcasted_iota(jnp.int32, (TOK, 128), 1) < HEAD_DIM
    zero = jnp.zeros((TOK, 128), BF)
    for block in range(STEP // TOK):
        rows = slice(block * TOK, (block + 1) * TOK)
        allowed = mask_ref[rows] > 0.5
        out = jnp.zeros((TOK, 128), F32)
        for head in range(2):
            mine = first if head == 0 else jnp.logical_not(first)
            scores = dot_nt(jnp.where(mine, q[rows], zero), k[rows]) * HEAD_DIM**-0.5
            scores = jnp.where(allowed, scores, -1e30)
            raised = jnp.exp(scores - jnp.max(scores, axis=-1, keepdims=True))
            prob = raised / jnp.sum(raised, axis=-1, keepdims=True)
            prob_ref[block, head] = prob
            out = out + dot(prob.astype(BF), jnp.where(mine, v[rows], zero))
        o_ref[rows] = out.astype(BF)


def inner(blocks, wa, masks):
    return pl.pallas_call(
        inner_kernel,
        grid=(ROWS // STEP,),
        in_specs=[whole_spec((TOK, D))] * REPS + [WA_SPEC] + [row_spec(128)] * 4,
        out_specs=[row_spec(D), row_spec(QKV_R), PROB_SPEC, row_spec(128), row_spec(FF_R), row_spec(FF_R), VEC_SPEC],
        out_shape=[
            rows_of(D, BF),
            rows_of(QKV_R, BF),
            jax.ShapeDtypeStruct((REPS, 2, TOK, TOK), F32),
            rows_of(128, BF),
            rows_of(FF_R, BF),
            rows_of(FF_R, F32),
            jax.ShapeDtypeStruct((16, D), F32),
        ],
        compiler_params=params(),
        name="inner",
    )(*blocks, wa, *masks)


HALF = jax.ShapeDtypeStruct((ROWS // 2, D), BF)


def outer_kernel(o_ref, act_ref, wo_ref, wd_ref, near_ref, far_ref):
    part = dot(o_ref[...], wo_ref[...]) + dot(act_ref[...], wd_ref[...])
    put_block(near_ref, far_ref, part.astype(BF))


def outer(attended, act, wo, wd):
    return pl.pallas_call(
        outer_kernel,
        grid=(ROWS // STEP,),
        in_specs=[row_spec(128), row_spec(FF_R), WO_SPEC, WD_SPEC],
        out_specs=[NEAR_SPEC, FAR_SPEC],
        out_shape=[HALF, HALF],
        compiler_params=params(),
        name="outer",
    )(attended, act, wo, wd)


def backward_kernel(
    e_ref, xh_ref, qkv_ref, prob_ref, slope_ref, wa_ref, wd_ref, wo_ref, vec_ref, cos_ref, low_ref, high_ref,
    near_ref, far_ref, dc_ref, du_ref, side_ref,
):
    def add_row(at, values):
        for j in range(values.shape[1] // 128):
            side_ref[at + j : at + j + 1] += values[:, 128 * j : 128 * (j + 1)]

    @pl.when(pl.program_id(0) == 0)
    def _():
        side_ref[...] = jnp.zeros_like(side_ref)

    e = e_ref[...]
    add_row(32, jnp.sum(e.astype(F32), axis=0, keepdims=True))
    du = (dot_nt(e, wd_ref[...]) * slope_ref[...]).astype(BF)
    du_ref[...] = du
    grad_o = dot_nt(e, wo_ref[...]).astype(BF)
    tables = (cos_ref[...], low_ref[...], high_ref[...])
    first = lax.broadcasted_iota(jnp.int32, (TOK, 128), 1) < HEAD_DIM
    zero = jnp.zeros((TOK, 128), BF)
    grads = ([], [], [])
    for block in range(STEP // TOK):
        rows = slice(block * TOK, (block + 1) * TOK)
        q, k, v = qkv_ref[rows, :128], qkv_ref[rows, 128:256], qkv_ref[rows, 256:]
        dq = jnp.zeros((TOK, 128), F32)
        dk = jnp.zeros((TOK, 128), F32)
        dv = jnp.zeros((TOK, 128), F32)
        for head in range(2):
            mine = first if head == 0 else jnp.logical_not(first)
            prob = prob_ref[block, head]
            grad_head = jnp.where(mine, grad_o[rows], zero)
            dv = dv + dot_tn(prob.astype(BF), grad_head)
            grad_prob = dot_nt(grad_head, v)
            inner_sum = jnp.sum(prob * grad_prob, axis=-1, keepdims=True)
            ds = (prob * (grad_prob - inner_sum)).astype(BF)
            dq = dq + dot(ds, jnp.where(mine, k, zero))
            dk = dk + dot_tn(ds, jnp.where(mine, q, zero))
        grads[0].append(dq * HEAD_DIM**-0.5)
        grads[1].append(dk * HEAD_DIM**-0.5)
        grads[2].append(dv)
    dq, dk, dv = (jnp.concatenate(g, axis=0) for g in grads)
    dc = jnp.concatenate([turn_back(dq, *tables), turn_back(dk, *tables), dv], axis=1).astype(BF)
    dc_ref[...] = dc
    dh1 = dot_nt(dc, wa_ref[:, :QKV_R])
    dh2 = dot_nt(du, wa_ref[:, QKV_R:A_LANES])
    put_block(near_ref, far_ref, (dh1 * vec_ref[0:1] + dh2 * vec_ref[2:3]).astype(BF))
    xh = xh_ref[...].astype(F32)
    add_row(0, jnp.sum(dh1 * xh, axis=0, keepdims=True))
    add_row(8, jnp.sum(dh1, axis=0, keepdims=True))
    add_row(16, jnp.sum(dh2 * xh, axis=0, keepdims=True))
    add_row(24, jnp.sum(dh2, axis=0, keepdims=True))
    add_row(40, jnp.sum(dc.astype(F32), axis=0, keepdims=True))
    add_row(43, jnp.sum(du.astype(F32), axis=0, keepdims=True))


def backward(e, kept, weights, masks):
    xh, qkv, prob, _, _, slope, vectors = kept
    return pl.pallas_call(
        backward_kernel,
        grid=(ROWS // STEP,),
        in_specs=[row_spec(D), row_spec(D), row_spec(QKV_R), PROB_SPEC, row_spec(FF_R)]
        + [WA_SPEC, WD_SPEC, WO_SPEC, VEC_SPEC]
        + [row_spec(128)] * 3,
        out_specs=[NEAR_SPEC, FAR_SPEC, row_spec(QKV_R), row_spec(FF_R), whole_spec((64, 128))],
        out_shape=[
            HALF,
            HALF,
            rows_of(QKV_R, BF),
            rows_of(FF_R, BF),
            jax.ShapeDtypeStruct((64, 128), F32),
        ],
        compiler_params=params(),
        name="backward",
    )(e, xh, qkv, prob, slope, *weights, vectors, *masks[1:])


def grad_in_kernel(xh_ref, vec_ref, dc_ref, du_ref, side_ref, out_ref):
    xh = xh_ref[...].astype(F32)
    h1 = (xh * vec_ref[0:1] + vec_ref[1:2]).astype(BF)
    h2 = (xh * vec_ref[2:3] + vec_ref[3:4]).astype(BF)
    out_ref[:, :, :QKV_R] = dot_tn(h1, dc_ref[...]).astype(BF).reshape(4, 64, QKV_R)
    out_ref[:, :, QKV_R:A_LANES] = dot_tn(h2, du_ref[...]).astype(BF).reshape(4, 64, FF_R)
    out_ref[:, :, A_LANES:] = jnp.broadcast_to(side_ref[...].astype(BF)[None], (4, 64, 128))


def grad_in(xh, vectors, dc, du, side):
    return pl.pallas_call(
        grad_in_kernel,
        grid=(4,),
        in_specs=[
            pl.BlockSpec((ROWS, 256), lambda i: (0, i)),
            pl.BlockSpec((16, 256), lambda i: (0, i)),
            whole_spec((ROWS, QKV_R)),
            whole_spec((ROWS, FF_R)),
            whole_spec((64, 128)),
        ],
        out_specs=pl.BlockSpec((4, 64, D), lambda i: (i, 0, 0)),
        out_shape=jax.ShapeDtypeStruct((SHARDS, 64, D), BF),
        compiler_params=params(),
        name="grad_in",
    )(xh, vectors, dc, du, side)


def grad_out_kernel(o_ref, act_ref, *refs):
    pieces, (out_ref, e_ref) = refs[:REPS], refs[REPS:]
    e = jnp.concatenate([piece[...] for piece in pieces], axis=0)
    e_ref[...] = e
    down = dot_tn(act_ref[...], e).reshape(SHARDS, UNIT, 256)
    dense = dot_tn(o_ref[...], e).reshape(SHARDS, 8, 256)
    empty = jnp.zeros((SHARDS, 8, 256), F32)
    out_ref[...] = jnp.concatenate([down, dense, empty], axis=1).astype(BF)


def grad_out_of(attended, act, blocks):
    return pl.pallas_call(
        grad_out_kernel,
        grid=(4,),
        in_specs=[
            whole_spec((ROWS, 128)),
            whole_spec((ROWS, FF_R)),
        ]
        + [pl.BlockSpec((TOK, 256), lambda i: (0, i))] * REPS,
        out_specs=[
            pl.BlockSpec((SHARDS, 48, 256), lambda i: (0, 0, i)),
            pl.BlockSpec((ROWS, 256), lambda i: (0, i)),
        ],
        out_shape=[jax.ShapeDtypeStruct((SHARDS, 48, D), BF), rows_of(D, BF)],
        compiler_params=params(),
        name="grad_out",
    )(attended, act, *blocks)


def standardize(x):
    centered = x - jnp.mean(x, axis=-1, keepdims=True)
    scale = lax.rsqrt(jnp.mean(centered * centered, axis=-1, keepdims=True) + EPS)
    return centered * scale, scale


def token_tables(docs):
    slot = np.arange(TOK)
    same = docs[:, :, None] == docs[:, None, :]
    mask = (same & (slot[None, :] <= slot[:, None])).astype(F32)
    places = jnp.sum(mask, axis=2) - 1.0
    angle = np.arange(TOK, dtype=np.float64)[:, None] * (10000.0 ** (-2.0 * np.arange(8) / ROT))[None, :]
    lane = np.arange(128) % HEAD_DIM
    cos_n = np.where(lane[None, :] < ROT, np.cos(angle)[:, lane % 8], 1.0)
    low_n = np.where(lane[None, :] < 8, -np.sin(angle)[:, lane % 8], 0.0)
    high_n = np.where((lane[None, :] >= 8) & (lane[None, :] < ROT), np.sin(angle)[:, lane % 8], 0.0)
    table = np.concatenate([cos_n, low_n, high_n], axis=1).astype(np.float32)
    chosen = (places.reshape(ROWS, 1) == slot[None, :].astype(np.float32)).astype(F32)
    found = jnp.dot(chosen, jnp.asarray(table), precision=lax.Precision.HIGHEST)
    return (mask.reshape(ROWS, TOK), found[:, :128], found[:, 128:256], found[:, 256:])


def in_order(near, far, c):
    return jnp.stack([jnp.where(c == 0, near, far), jnp.where(c == 0, far, near)], axis=1).reshape((REPS,) + near.shape[1:])


def per_device(
    tokens, doc_ids, grad_out, norm_gains, shifts, qkv_weight, qkv_bias, dense_weight, up_weight, up_bias, down_weight
):
    r = lax.axis_index("rep").astype(jnp.int32)
    s = lax.axis_index("shard").astype(jnp.int32)
    y, c = r // 2, r % 2
    place = jnp.stack([r, s])

    vectors = jnp.concatenate([norm_gains, shifts, qkv_bias.reshape(LAYERS, 3, 64)], axis=1)
    slots = jnp.concatenate([jnp.tile(vectors, (1, 1, 2)), up_bias.reshape(LAYERS, 2, 128)], axis=1)
    slots = jnp.pad(slots.astype(F32), ((0, 0), (0, 5), (0, 0)))
    packed_a, packed_b = pack(place, qkv_weight, up_weight, down_weight, slots)
    wa0 = gather_shard(packed_a[0]).reshape(D, D)

    current = tokens.astype(F32)
    hat, scale = standardize(current)
    marks = jnp.pad(doc_ids.astype(BF).reshape(1, TOK), ((0, 15), (0, D - TOK)))
    opened = gather_rep(jnp.concatenate([hat.astype(BF), marks], axis=0))
    masks = token_tables(jnp.stack([piece[TOK, :TOK] for piece in opened]).astype(F32))
    live = (doc_ids >= 0).astype(F32)[:, None]
    grad_y = grad_out.astype(F32) * live
    low, opened = lax.optimization_barrier((grad_y.astype(BF), opened))
    top = gather_rep(low)

    wo = gather_dense(dense_weight, s)
    wd0 = gather_shard(packed_b[0]).reshape(FF_R, D)
    late, wa0 = lax.optimization_barrier((jnp.concatenate([packed_a[1], packed_b[1]], axis=0), wa0))
    late = lax.all_gather(late, "shard", axis=0)
    weights = [(wa0, wd0, wo[0]), (late[:, :64].reshape(D, D), late[:, 64:].reshape(FF_R, D), wo[1])]

    kept, hats, scales = [], [], []
    for number in range(LAYERS):
        blocks = opened
        if number:
            hat, scale = standardize(current)
            blocks = gather_rep(hat.astype(BF))
        wa, wd, wo_here = weights[number]
        saved = inner(blocks, wa, masks)
        part = outer(saved[3], saved[4], wo_here, wd)
        current = current + scatter_rep(*part) + saved[6][4:5] + saved[6][5:6]
        kept.append(saved)
        hats.append(hat)
        scales.append(scale)
    output = current.astype(BF)

    pieces = [None] * LAYERS
    sums_above = None
    for number in reversed(range(LAYERS)):
        saved = kept[number]
        blocks = top
        if number < LAYERS - 1:
            blocks = gather_rep(grad_y.astype(BF))
            blocks, sums_above = lax.optimization_barrier((blocks, sums_above))
            near, far = gather_rep_ordered(sums_above, y)
            pieces[number + 1] = (near[:, :64], far[:, :64], near[:, 64:], far[:, 64:])
        shares, e = grad_out_of(saved[3], saved[4], blocks)
        sum_b = scatter_shard(shares)
        moved = lax.ppermute(sum_b[UNIT:], ("rep", "shard"), DENSE_OUT)
        sum_b = jnp.concatenate([sum_b[:UNIT], moved], axis=0)
        *part, dc, du, side = backward(e, saved, weights[number], masks)
        total = scatter_rep(*part)
        sum_a = scatter_shard(grad_in(saved[0], saved[6], dc, du, side))
        if number:
            sums_above = jnp.concatenate([sum_a, sum_b], axis=0)
        else:
            pieces[number] = (*gather_rep_at_once(sum_a), *gather_rep_ordered(sum_b, y))

        hat = hats[number]
        shared = jnp.mean(total, axis=-1, keepdims=True)
        along = jnp.mean(total * hat, axis=-1, keepdims=True)
        grad_y = grad_y + scales[number] * (total - shared - hat * along)

    grad_qkv, grad_up, grad_down, grad_dense = unpack(place, *pieces[0], *pieces[1])

    sides = [in_order(p[0][:, :47, A_LANES:], p[1][:, :47, A_LANES:], c).astype(F32) for p in pieces]
    side = jnp.stack(sides)
    sums = jnp.sum(side[:, :, :32], axis=1)
    sums = jnp.concatenate([sums, side[:, 0, 32:40]], axis=1).reshape(LAYERS, 5, D)
    sums = lax.dynamic_slice_in_dim(sums, 64 * s, 64, 2)
    grad_gains = jnp.stack([sums[:, 0], sums[:, 2]], axis=1)
    grad_shifts = jnp.stack([sums[:, 1], sums[:, 3], sums[:, 4], sums[:, 4]], axis=1)
    qkv_b = jnp.swapaxes(side[:, :, 40:43], 1, 2).reshape(LAYERS, 3 * D)
    grad_qkv_bias = lax.dynamic_slice_in_dim(qkv_b, 192 * s, 192, 1)
    up_b = side[:, :, 43:].reshape(LAYERS, REPS, FF_R)
    grad_up_bias = lax.dynamic_slice_in_dim(up_b, UNIT * s, UNIT, 2).reshape(LAYERS, 256)
    return (
        output,
        grad_y,
        grad_gains,
        grad_shifts,
        grad_qkv,
        grad_qkv_bias,
        grad_dense,
        grad_up,
        grad_up_bias,
        grad_down,
    )


def solution(mesh):
    return jax.shard_map(
        per_device,
        mesh=mesh,
        in_specs=(
            P(("rep", "shard"), None),
            P(("rep", "shard")),
            P(("rep", "shard"), None),
            P(None, None, "shard"),
            P(None, None, "shard"),
            P(None, "shard", None),
            P(None, "shard"),
            P(None, "shard", None),
            P(None, "shard", None),
            P(None, "shard"),
            P(None, "shard", None),
        ),
        out_specs=(
            P(("rep", "shard"), None),
            P(("rep", "shard"), None),
            P(None, None, "shard"),
            P(None, None, "shard"),
            P(None, "shard", None),
            P(None, "shard"),
            P(None, "shard", None),
            P(None, "shard", None),
            P(None, "shard"),
            P(None, "shard", None),
        ),
        check_vma=False,
    )
```

```python
import math

import jax
import jax.numpy as jnp
import numpy as np
from jax import lax
from jax.experimental import pallas as pl
from jax.experimental.pallas import tpu as pltpu
from jax.sharding import PartitionSpec as P

HEADS = 16
HEAD_DIM = 64
ROT = 16
LAYERS = 2
D = 1024
FF = 4096
TOK = 128
REPS = 8
SHARDS = 16
ROWS = REPS * TOK
QKV_R = 3 * D // REPS
FF_R = FF // REPS
A_LANES = QKV_R + FF_R
UNIT = FF // SHARDS // REPS
STEP = 256
EPS = 1e-05
LARGE = 58 * 2**20
SMALL = 24 * 2**20

BF = jnp.bfloat16
F32 = jnp.float32


def take_y(k):
    return [(((y + k) % 4) * 2 + c, y * 2 + c) for y in range(4) for c in range(2)]


CORE_FLIP = [(y * 2 + 1 - c, y * 2 + c) for y in range(4) for c in range(2)]


def fetch_y(a, k):
    return lax.ppermute(a, "rep", take_y(k % 4))


def flip_core(a):
    return lax.ppermute(a, "rep", CORE_FLIP)


Y_GROUPS = [[0, 2, 4, 6], [1, 3, 5, 7]]


def along_y(a):
    return lax.all_to_all(a, "rep", 0, 0, axis_index_groups=Y_GROUPS, tiled=True)


def gather_rep(block):
    near = [block] + [fetch_y(block, k) for k in (1, 2, 3)]
    return near + [flip_core(piece) for piece in near]


def in_y_order(pieces, y):
    near = jnp.zeros((4,) + pieces[0].shape, pieces[0].dtype)
    for k in range(4):
        near = lax.dynamic_update_slice_in_dim(near, pieces[k][None], (y + k) % 4, 0)
    return near


def scatter_rep(near, far):
    own, *sent = join(near, flip_core(far))
    return own, [fetch_y(sent[k - 1], -k) for k in (1, 2, 3)]


def total_of(own, moved):
    for piece in moved:
        own = own + piece.astype(F32)
    return own


def exchange_shard(a):
    return lax.all_to_all(a, "shard", 0, 0, tiled=True)


def add_up(pieces):
    return jnp.sum(pieces.astype(F32), axis=0).astype(BF)


DENSE_IN = [((s % 8) * 16 + 2 * r + s // 8, r * 16 + s) for r in range(REPS) for s in range(SHARDS)]
DENSE_OUT = [((s // 2) * 16 + 8 * (s % 2) + r, r * 16 + s) for r in range(REPS) for s in range(SHARDS)]


def dot(a, b):
    return lax.dot_general(a, b, (((1,), (0,)), ((), ())), preferred_element_type=F32)


def dot_nt(a, b):
    return lax.dot_general(a, b, (((1,), (1,)), ((), ())), preferred_element_type=F32)


def dot_tn(a, b):
    return lax.dot_general(a, b, (((0,), (0,)), ((), ())), preferred_element_type=F32)


def params(limit=SMALL):
    return pltpu.CompilerParams(vmem_limit_bytes=limit)


VMEM = pl.BlockSpec(memory_space=pltpu.VMEM)
SMEM = pl.BlockSpec(memory_space=pltpu.SMEM)


def pack_kernel(place_ref, *refs):
    qkv_refs, up_refs, (down_ref, gains_ref, moves_ref, qkv_bias_ref, up_bias_ref, first_ref, a1_ref, b_ref, a_ref) = refs[:3], refs[3:19], refs[19:]
    r, s = place_ref[0], place_ref[1]
    lane = lax.broadcasted_iota(jnp.int32, (64, 128), 1)
    row = lax.broadcasted_iota(jnp.int32, (64, 128), 0)
    for layer in range(LAYERS):
        for part in range(3):
            a_ref[layer, :, part * 128 : (part + 1) * 128] = qkv_refs[part][layer]
        for group in range(4):
            merged = jnp.zeros((64, 128), F32)
            for sub in range(4):
                piece = up_refs[4 * group + sub][layer].astype(F32)
                turned = pltpu.roll(piece, (32 * sub + 128 - 32 * (r % 4)) % 128, 1)
                merged = jnp.where(lane // 32 == sub, turned, merged)
            low = QKV_R + group * 128
            a_ref[layer, :, low : low + 128] = merged.astype(BF)
        b_ref[layer] = down_ref[layer]
        gains, moves = gains_ref[layer].astype(F32), moves_ref[layer].astype(F32)
        bias = qkv_bias_ref[layer : layer + 1].astype(F32)
        side = jnp.zeros((64, 128), F32)
        for vector, values in enumerate((gains[0:1], moves[0:1], gains[1:2], moves[1:2], moves[2:3], moves[3:4])):
            here = (row == 8 * vector + s // 2) & (lane // 64 == s % 2)
            side = jnp.where(here, jnp.concatenate([values, values], axis=1), side)
        for third in range(3):
            block = 3 * s + third
            target = jnp.where((block // 2) % 8 == r, 48 + block // 16, -1)
            here = (row == target) & (lane // 64 == block % 2)
            values = bias[:, 64 * third : 64 * (third + 1)]
            side = jnp.where(here, jnp.concatenate([values, values], axis=1), side)
        bias = up_bias_ref[layer : layer + 1].astype(F32)
        piece = jnp.where(r // 4 == 0, bias[:, :128], bias[:, 128:])
        turned = pltpu.roll(jnp.broadcast_to(piece, (64, 128)), (32 * (s % 4) + 128 - 32 * (r % 4)) % 128, 1)
        side = jnp.where((row == 51 + s // 4) & (lane // 32 == s % 4), turned, side)
        a_ref[layer, :, A_LANES:] = side.astype(BF)
    first_ref[...] = jnp.broadcast_to(a_ref[0][None], (SHARDS, 64, D))
    a1_ref[...] = a_ref[1]


def pack(place, qkv_weight, up_weight, down_weight, *vectors):
    def lanes(at):
        return pl.BlockSpec((LAYERS, 64, 128), lambda i, place: (0, 0, at(place[0])))

    def whole(a):
        return pl.BlockSpec(a.shape, lambda i, place: (0,) * a.ndim)

    return pl.pallas_call(
        pack_kernel,
        grid_spec=pltpu.PrefetchScalarGridSpec(
            num_scalar_prefetch=1,
            grid=(1,),
            in_specs=[lanes(lambda r, p=p: 8 * p + r) for p in range(3)]
            + [lanes(lambda r, o=o: 2 * o + r // 4) for o in range(16)]
            + [pl.BlockSpec((LAYERS, UNIT, D), lambda i, place: (0, place[0], 0))]
            + [whole(a) for a in vectors],
            out_specs=[
                pl.BlockSpec((SHARDS, 64, D), lambda i, place: (0, 0, 0)),
                pl.BlockSpec((64, D), lambda i, place: (0, 0)),
                pl.BlockSpec((LAYERS, UNIT, D), lambda i, place: (0, 0, 0)),
            ],
            scratch_shapes=[pltpu.VMEM((LAYERS, 64, D), BF)],
        ),
        out_shape=[
            jax.ShapeDtypeStruct((SHARDS, 64, D), BF),
            jax.ShapeDtypeStruct((64, D), BF),
            jax.ShapeDtypeStruct((LAYERS, UNIT, D), BF),
        ],
        compiler_params=params(LARGE),
        name="pack",
    )(place, *[qkv_weight] * 3, *[up_weight] * 16, down_weight, *vectors)


def put_inside(piece, r, qkv_ref, layer):
    for part in range(3):
        low = part * D + 128 * r
        qkv_ref[layer, :, low : low + 128] = piece[:, part * 128 : (part + 1) * 128]


def put_up(whole, up_ref, layer):
    lane = lax.broadcasted_iota(jnp.int32, (64, 128), 1)
    for s in range(SHARDS):
        group, sub = s // 4, s % 4
        for half in range(2):
            merged = jnp.zeros((64, 128), F32)
            for inner_r in range(4):
                piece = whole[4 * half + inner_r][:, group * 128 : (group + 1) * 128]
                shift = (32 * inner_r - 32 * sub) % 128
                turned = pltpu.roll(piece, shift, 1) if shift else piece
                merged = jnp.where(lane // 32 == inner_r, turned, merged)
            low = 256 * s + 128 * half
            up_ref[layer, :, low : low + 128] = merged


def put_layer(place_ref, near_ref, far_ref, qkv_ref, up_ref, down_ref, dense_ref=None):
    c = place_ref[0] % 2
    whole = []
    for r in range(REPS):
        piece = jnp.where(c == r % 2, near_ref[r // 2], far_ref[r // 2]).astype(F32)
        put_inside(piece[:64], r, qkv_ref, 0)
        whole.append(piece[:64, QKV_R:A_LANES])
        down_ref[0, UNIT * r : UNIT * (r + 1), :] = piece[64:96]
        if dense_ref is not None:
            dense_ref[1, 8 * r : 8 * r + 8, :] = piece[96:104]
            dense_ref[0, 8 * r : 8 * r + 8, :] = piece[112:120]
    put_up(whole, up_ref, 0)


def unpack_late_kernel(place_ref, near_ref, far_ref, qkv_in, up_in, down_in, *out_refs):
    put_layer(place_ref, near_ref, far_ref, *out_refs)


UNPACKED = [
    jax.ShapeDtypeStruct((LAYERS, 64, 3 * D), F32),
    jax.ShapeDtypeStruct((LAYERS, 64, FF), F32),
    jax.ShapeDtypeStruct((LAYERS, 256, D), F32),
]


def layer_specs(layer):
    return [pl.BlockSpec((1,) + a.shape[1:], lambda i: (layer, 0, 0)) for a in UNPACKED]


def unpack_early(place, near, far):
    return pl.pallas_call(
        put_layer,
        grid=(1,),
        in_specs=[SMEM, VMEM, VMEM],
        out_specs=layer_specs(1),
        out_shape=UNPACKED,
        compiler_params=params(),
        name="unpack_early",
    )(place, near, far)


def unpack_late(place, near, far, *filled):
    return pl.pallas_call(
        unpack_late_kernel,
        grid=(1,),
        in_specs=[SMEM, VMEM, VMEM] + [pl.BlockSpec(memory_space=pl.ANY)] * 3,
        out_specs=layer_specs(0) + [VMEM],
        out_shape=UNPACKED + [jax.ShapeDtypeStruct((LAYERS, 64, D), F32)],
        input_output_aliases={3: 0, 4: 1, 5: 2},
        compiler_params=params(),
        name="unpack_late",
    )(place, near, far, *filled)


def join_kernel(near_ref, far_ref, own_ref, *sent_refs):
    for k in range(4):
        rows = slice(k * TOK, (k + 1) * TOK)
        both = near_ref[rows].astype(F32) + far_ref[rows].astype(F32)
        if k == 0:
            own_ref[...] = both
        else:
            sent_refs[k - 1][...] = both.astype(BF)


def join(near, far):
    sent = jax.ShapeDtypeStruct((TOK, D), BF)
    return pl.pallas_call(
        join_kernel,
        in_specs=[VMEM, VMEM],
        out_specs=[VMEM] * 4,
        out_shape=[jax.ShapeDtypeStruct((TOK, D), F32), sent, sent, sent],
        compiler_params=params(),
        name="join",
    )(near, far)


def rotary_table():
    angle = np.arange(TOK, dtype=np.float64)[:, None] * (10000.0 ** (-2.0 * np.arange(8) / ROT))[None, :]
    lane = np.arange(128) % HEAD_DIM
    cos_n = np.where(lane[None, :] < ROT, np.cos(angle)[:, lane % 8], 1.0)
    low_n = np.where(lane[None, :] < 8, -np.sin(angle)[:, lane % 8], 0.0)
    high_n = np.where((lane[None, :] >= 8) & (lane[None, :] < ROT), np.sin(angle)[:, lane % 8], 0.0)
    rest = np.concatenate([cos_n, low_n, high_n], axis=1).astype(np.float32)
    parts = []
    for _ in range(3):
        parts.append(rest.astype(BF))
        rest = rest - parts[-1].astype(np.float32)
    return np.stack(parts)


def tables_kernel(table_ref, *refs):
    pieces, (mask_ref, cos_ref, low_ref, high_ref) = refs[:REPS], refs[REPS:]
    row = lax.broadcasted_iota(jnp.int32, (TOK, TOK), 0)
    col = lax.broadcasted_iota(jnp.int32, (TOK, TOK), 1)
    for block in range(REPS):
        rows = slice(block * TOK, (block + 1) * TOK)
        docs = jnp.broadcast_to(pieces[block][...].astype(F32)[0:1], (TOK, TOK))
        mask = jnp.where((docs == docs.T) & (col <= row), 1.0, 0.0)
        mask_ref[rows] = mask
        places = jnp.sum(mask, axis=1, keepdims=True) - 1.0
        chosen = jnp.where(col.astype(F32) == places, 1.0, 0.0).astype(BF)
        found = dot(chosen, table_ref[0]) + dot(chosen, table_ref[1]) + dot(chosen, table_ref[2])
        cos_ref[rows] = found[:, :128]
        low_ref[rows] = found[:, 128:256]
        high_ref[rows] = found[:, 256:]


def token_tables(opened):
    return pl.pallas_call(
        tables_kernel,
        grid=(1,),
        in_specs=[VMEM] + [pl.BlockSpec((16, 128), lambda i: (16, 0))] * REPS,
        out_specs=[VMEM] * 4,
        out_shape=[jax.ShapeDtypeStruct((ROWS, 128), F32)] * 4,
        compiler_params=params(),
        name="tables",
    )(jnp.asarray(rotary_table()), *opened)


def turn(values, cos_t, low_t, high_t):
    return values * cos_t + pltpu.roll(values, 120, 1) * low_t + pltpu.roll(values, 8, 1) * high_t


def turn_back(values, cos_t, low_t, high_t):
    return values * cos_t - pltpu.roll(values, 120, 1) * low_t - pltpu.roll(values, 8, 1) * high_t


def row_spec(lanes):
    return pl.BlockSpec((STEP, lanes), lambda i: (i, 0))


def whole_spec(shape):
    return pl.BlockSpec(shape, lambda i: (0,) * len(shape))


PROB_SPEC = pl.BlockSpec((STEP // TOK, 2, TOK, TOK), lambda i: (i, 0, 0, 0))
WA_SPEC = whole_spec((SHARDS, 64, D))
HELD = [pltpu.VMEM((FF_R, D), BF), pltpu.VMEM((128, D), BF)]


def wb_specs(at):
    return [pl.BlockSpec((SHARDS, 16, D), lambda i, k=k: (0, at + k, 0)) for k in range(3)]


def hold_weights(wb_refs, wd_ref, wo_ref):
    @pl.when(pl.program_id(0) == 0)
    def _():
        rows = jnp.concatenate([wb_refs[0][...], wb_refs[1][...]], axis=1)
        wd_ref[...] = rows.reshape(FF_R, D)
        wo_ref[...] = wb_refs[2][...].astype(F32)[:, :8].reshape(128, D).astype(BF)


VEC_SPEC = whole_spec((16, D))
NEAR_SPEC = pl.BlockSpec((STEP, D), lambda i: (jnp.minimum(i, 1), 0))
FAR_SPEC = pl.BlockSpec((STEP, D), lambda i: (jnp.maximum(i - 2, 0), 0))


def rows_of(lanes, dtype):
    return jax.ShapeDtypeStruct((ROWS, lanes), dtype)


def put_block(near_ref, far_ref, values):
    @pl.when(pl.program_id(0) < 2)
    def _():
        near_ref[...] = values

    @pl.when(pl.program_id(0) >= 2)
    def _():
        far_ref[...] = values


def inner_kernel(*refs):
    pieces, (wa_ref, mask_ref, cos_ref, low_ref, high_ref) = refs[:REPS], refs[REPS : REPS + 5]
    xh_ref, qkv_ref, prob_ref, o_ref, act_ref, slope_ref, vec_ref = refs[REPS + 5 :]

    @pl.when(pl.program_id(0) == 0)
    def _():
        side = jnp.zeros((64, 128), F32)
        for shard in range(SHARDS):
            side = side + wa_ref[shard, :, A_LANES:].astype(F32)
        vec_ref[...] = jnp.zeros_like(vec_ref)
        for vector in range(6):
            for j in range(8):
                vec_ref[vector : vector + 1, 128 * j : 128 * (j + 1)] = side[8 * vector + j : 8 * vector + j + 1]
        for j in range(7):
            vec_ref[6:7, 128 * j : 128 * (j + 1)] = side[48 + j : 49 + j]

    for step in range(4):

        @pl.when(pl.program_id(0) == step)
        def _(step=step):
            xh_ref[:TOK] = pieces[2 * step][...]
            xh_ref[TOK:] = pieces[2 * step + 1][...]

    xh = xh_ref[...].astype(F32)
    h1 = (xh * vec_ref[0:1] + vec_ref[1:2]).astype(BF)
    h2 = (xh * vec_ref[2:3] + vec_ref[3:4]).astype(BF)
    mixed = dot(h1, wa_ref[:, :, :QKV_R].reshape(D, QKV_R)) + vec_ref[6:7, :QKV_R]
    tables = (cos_ref[...], low_ref[...], high_ref[...])
    q = turn(mixed[:, :128], *tables).astype(BF)
    k = turn(mixed[:, 128:256], *tables).astype(BF)
    v = mixed[:, 256:].astype(BF)
    qkv_ref[:, :128] = q
    qkv_ref[:, 128:256] = k
    qkv_ref[:, 256:] = v
    u = dot(h2, wa_ref[:, :, QKV_R:A_LANES].reshape(D, FF_R)) + vec_ref[6:7, QKV_R:A_LANES]
    share = 0.5 * (1.0 + lax.erf(u * math.sqrt(0.5)))
    act_ref[...] = (u * share).astype(BF)
    slope_ref[...] = share + u * jnp.exp(-0.5 * u * u) * (1.0 / math.sqrt(2.0 * math.pi))
    first = lax.broadcasted_iota(jnp.int32, (TOK, 128), 1) < HEAD_DIM
    zero = jnp.zeros((TOK, 128), BF)
    for block in range(STEP // TOK):
        rows = slice(block * TOK, (block + 1) * TOK)
        allowed = mask_ref[rows] > 0.5
        out = jnp.zeros((TOK, 128), F32)
        for head in range(2):
            mine = first if head == 0 else jnp.logical_not(first)
            scores = dot_nt(jnp.where(mine, q[rows], zero), k[rows]) * HEAD_DIM**-0.5
            scores = jnp.where(allowed, scores, -1e30)
            raised = jnp.exp(scores - jnp.max(scores, axis=-1, keepdims=True))
            prob = raised / jnp.sum(raised, axis=-1, keepdims=True)
            prob_ref[block, head] = prob
            out = out + dot(prob.astype(BF), jnp.where(mine, v[rows], zero))
        o_ref[rows] = out.astype(BF)


def inner(blocks, wa, masks):
    return pl.pallas_call(
        inner_kernel,
        grid=(ROWS // STEP,),
        in_specs=[whole_spec((TOK, D))] * REPS + [WA_SPEC] + [row_spec(128)] * 4,
        out_specs=[row_spec(D), row_spec(QKV_R), PROB_SPEC, row_spec(128), row_spec(FF_R), row_spec(FF_R), VEC_SPEC],
        out_shape=[
            rows_of(D, BF),
            rows_of(QKV_R, BF),
            jax.ShapeDtypeStruct((REPS, 2, TOK, TOK), F32),
            rows_of(128, BF),
            rows_of(FF_R, BF),
            rows_of(FF_R, F32),
            jax.ShapeDtypeStruct((16, D), F32),
        ],
        compiler_params=params(LARGE),
        name="inner",
    )(*blocks, wa, *masks)


HALF = jax.ShapeDtypeStruct((ROWS // 2, D), BF)


def outer_kernel(o_ref, act_ref, down0_ref, down1_ref, dense_ref, near_ref, far_ref, wd_ref, wo_ref):
    hold_weights((down0_ref, down1_ref, dense_ref), wd_ref, wo_ref)
    part = dot(o_ref[...], wo_ref[...]) + dot(act_ref[...], wd_ref[...])
    put_block(near_ref, far_ref, part.astype(BF))


def outer(attended, act, wb, at):
    return pl.pallas_call(
        outer_kernel,
        grid=(ROWS // STEP,),
        in_specs=[row_spec(128), row_spec(FF_R)] + wb_specs(at),
        out_specs=[NEAR_SPEC, FAR_SPEC],
        out_shape=[HALF, HALF],
        scratch_shapes=HELD,
        compiler_params=params(),
        name="outer",
    )(attended, act, wb, wb, wb)


def backward_kernel(
    e_ref, xh_ref, qkv_ref, prob_ref, slope_ref, wa_ref, down0_ref, down1_ref, dense_ref, vec_ref, cos_ref, low_ref, high_ref,
    near_ref, far_ref, dc_ref, du_ref, side_ref, wd_ref, wo_ref,
):
    def add_row(at, values):
        for j in range(values.shape[1] // 128):
            side_ref[at + j : at + j + 1] += values[:, 128 * j : 128 * (j + 1)]

    @pl.when(pl.program_id(0) == 0)
    def _():
        side_ref[...] = jnp.zeros_like(side_ref)

    hold_weights((down0_ref, down1_ref, dense_ref), wd_ref, wo_ref)
    e = e_ref[...]
    add_row(32, jnp.sum(e.astype(F32), axis=0, keepdims=True))
    du = (dot_nt(e, wd_ref[...]) * slope_ref[...]).astype(BF)
    du_ref[...] = du
    grad_o = dot_nt(e, wo_ref[...]).astype(BF)
    tables = (cos_ref[...], low_ref[...], high_ref[...])
    first = lax.broadcasted_iota(jnp.int32, (TOK, 128), 1) < HEAD_DIM
    zero = jnp.zeros((TOK, 128), BF)
    grads = ([], [], [])
    for block in range(STEP // TOK):
        rows = slice(block * TOK, (block + 1) * TOK)
        q, k, v = qkv_ref[rows, :128], qkv_ref[rows, 128:256], qkv_ref[rows, 256:]
        dq = jnp.zeros((TOK, 128), F32)
        dk = jnp.zeros((TOK, 128), F32)
        dv = jnp.zeros((TOK, 128), F32)
        for head in range(2):
            mine = first if head == 0 else jnp.logical_not(first)
            prob = prob_ref[block, head]
            grad_head = jnp.where(mine, grad_o[rows], zero)
            dv = dv + dot_tn(prob.astype(BF), grad_head)
            grad_prob = dot_nt(grad_head, v)
            inner_sum = jnp.sum(prob * grad_prob, axis=-1, keepdims=True)
            ds = (prob * (grad_prob - inner_sum)).astype(BF)
            dq = dq + dot(ds, jnp.where(mine, k, zero))
            dk = dk + dot_tn(ds, jnp.where(mine, q, zero))
        grads[0].append(dq * HEAD_DIM**-0.5)
        grads[1].append(dk * HEAD_DIM**-0.5)
        grads[2].append(dv)
    dq, dk, dv = (jnp.concatenate(g, axis=0) for g in grads)
    dc = jnp.concatenate([turn_back(dq, *tables), turn_back(dk, *tables), dv], axis=1).astype(BF)
    dc_ref[...] = dc
    dh1 = dot_nt(dc, wa_ref[:, :, :QKV_R].reshape(D, QKV_R))
    dh2 = dot_nt(du, wa_ref[:, :, QKV_R:A_LANES].reshape(D, FF_R))
    put_block(near_ref, far_ref, (dh1 * vec_ref[0:1] + dh2 * vec_ref[2:3]).astype(BF))
    xh = xh_ref[...].astype(F32)
    add_row(0, jnp.sum(dh1 * xh, axis=0, keepdims=True))
    add_row(8, jnp.sum(dh1, axis=0, keepdims=True))
    add_row(16, jnp.sum(dh2 * xh, axis=0, keepdims=True))
    add_row(24, jnp.sum(dh2, axis=0, keepdims=True))
    add_row(40, jnp.sum(dc.astype(F32), axis=0, keepdims=True))
    add_row(43, jnp.sum(du.astype(F32), axis=0, keepdims=True))


def backward(e, kept, wa, wb, at, masks):
    xh, qkv, prob, _, _, slope, vectors = kept
    return pl.pallas_call(
        backward_kernel,
        grid=(ROWS // STEP,),
        in_specs=[row_spec(D), row_spec(D), row_spec(QKV_R), PROB_SPEC, row_spec(FF_R)]
        + [WA_SPEC]
        + wb_specs(at)
        + [VEC_SPEC]
        + [row_spec(128)] * 3,
        out_specs=[NEAR_SPEC, FAR_SPEC, row_spec(QKV_R), row_spec(FF_R), whole_spec((64, 128))],
        out_shape=[
            HALF,
            HALF,
            rows_of(QKV_R, BF),
            rows_of(FF_R, BF),
            jax.ShapeDtypeStruct((64, 128), F32),
        ],
        scratch_shapes=HELD,
        compiler_params=params(LARGE),
        name="backward",
    )(e, xh, qkv, prob, slope, wa, wb, wb, wb, vectors, *masks[1:])


def grad_in_kernel(xh_ref, vec_ref, dc_ref, du_ref, side_ref, out_ref):
    xh = xh_ref[...].astype(F32)
    h1 = (xh * vec_ref[0:1] + vec_ref[1:2]).astype(BF)
    h2 = (xh * vec_ref[2:3] + vec_ref[3:4]).astype(BF)
    out_ref[:, :, :QKV_R] = dot_tn(h1, dc_ref[...]).astype(BF).reshape(4, 64, QKV_R)
    out_ref[:, :, QKV_R:A_LANES] = dot_tn(h2, du_ref[...]).astype(BF).reshape(4, 64, FF_R)
    out_ref[:, :, A_LANES:] = jnp.broadcast_to(side_ref[...].astype(BF)[None], (4, 64, 128))


def grad_all_kernel(xh_ref, vec_ref, dc_ref, du_ref, side_ref, shares_ref, out_ref):
    grad_in_kernel(xh_ref, vec_ref, dc_ref, du_ref, side_ref, out_ref.at[:, :64])
    out_ref[:, 64:] = shares_ref[...]


def grad_all(xh, vectors, dc, du, side, shares):
    return pl.pallas_call(
        grad_all_kernel,
        grid=(4,),
        in_specs=[
            pl.BlockSpec((ROWS, 256), lambda i: (0, i)),
            pl.BlockSpec((16, 256), lambda i: (0, i)),
            whole_spec((ROWS, QKV_R)),
            whole_spec((ROWS, FF_R)),
            whole_spec((64, 128)),
            pl.BlockSpec((4, 48, D), lambda i: (i, 0, 0)),
        ],
        out_specs=pl.BlockSpec((4, 112, D), lambda i: (i, 0, 0)),
        out_shape=jax.ShapeDtypeStruct((SHARDS, 112, D), BF),
        compiler_params=params(),
        name="grad_all",
    )(xh, vectors, dc, du, side, shares)


def grad_in(xh, vectors, dc, du, side):
    return pl.pallas_call(
        grad_in_kernel,
        grid=(4,),
        in_specs=[
            pl.BlockSpec((ROWS, 256), lambda i: (0, i)),
            pl.BlockSpec((16, 256), lambda i: (0, i)),
            whole_spec((ROWS, QKV_R)),
            whole_spec((ROWS, FF_R)),
            whole_spec((64, 128)),
        ],
        out_specs=pl.BlockSpec((4, 64, D), lambda i: (i, 0, 0)),
        out_shape=jax.ShapeDtypeStruct((SHARDS, 64, D), BF),
        compiler_params=params(),
        name="grad_in",
    )(xh, vectors, dc, du, side)


def grad_out_kernel(o_ref, act_ref, *refs):
    pieces, (out_ref, e_ref) = refs[:REPS], refs[REPS:]
    e = jnp.concatenate([piece[...] for piece in pieces], axis=0)
    e_ref[...] = e
    down = dot_tn(act_ref[...], e).reshape(SHARDS, UNIT, 256)
    dense = dot_tn(o_ref[...], e).reshape(SHARDS, 8, 256)
    empty = jnp.zeros((SHARDS, 8, 256), F32)
    out_ref[...] = jnp.concatenate([down, dense, empty], axis=1).astype(BF)


def grad_out_of(attended, act, blocks, at):
    return pl.pallas_call(
        grad_out_kernel,
        grid=(4,),
        in_specs=[
            whole_spec((ROWS, 128)),
            whole_spec((ROWS, FF_R)),
        ]
        + [pl.BlockSpec((TOK, 256), lambda i: (at, i))] * REPS,
        out_specs=[
            pl.BlockSpec((SHARDS, 48, 256), lambda i: (0, 0, i)),
            pl.BlockSpec((ROWS, 256), lambda i: (0, i)),
        ],
        out_shape=[jax.ShapeDtypeStruct((SHARDS, 48, D), BF), rows_of(D, BF)],
        compiler_params=params(),
        name="grad_out",
    )(attended, act, *blocks)


def standardize(x):
    centered = x - jnp.mean(x, axis=-1, keepdims=True)
    scale = lax.rsqrt(jnp.mean(centered * centered, axis=-1, keepdims=True) + EPS)
    return centered * scale, scale


def in_order(near, far, c):
    return jnp.stack([jnp.where(c == 0, near, far), jnp.where(c == 0, far, near)], axis=1).reshape((REPS,) + near.shape[1:])


def per_device(
    tokens, doc_ids, grad_out, norm_gains, shifts, qkv_weight, qkv_bias, dense_weight, up_weight, up_bias, down_weight
):
    r = lax.axis_index("rep").astype(jnp.int32)
    s = lax.axis_index("shard").astype(jnp.int32)
    y, c = r // 2, r % 2
    place = jnp.stack([r, s])

    dense = lax.dynamic_slice_in_dim(dense_weight, 8 * r, 8, 1)
    dense = lax.ppermute(dense, ("rep", "shard"), DENSE_IN)
    first, late, packed_b = pack(place, qkv_weight, up_weight, down_weight, norm_gains, shifts, qkv_bias, up_bias)
    packed_b = jnp.concatenate([packed_b, dense, jnp.zeros((LAYERS, 8, D), BF)], axis=1)
    wa0 = exchange_shard(first)
    wb0 = lax.all_gather(packed_b[0], "shard", axis=0)

    current = tokens.astype(F32)
    hat, scale = standardize(current)
    live = (doc_ids >= 0).astype(F32)[:, None]
    grad_y = grad_out.astype(F32) * live
    marks = jnp.pad(doc_ids.astype(BF).reshape(1, TOK), ((0, 15), (0, D - TOK)))
    opened = gather_rep(jnp.concatenate([hat.astype(BF), grad_y.astype(BF), marks], axis=0))
    masks = token_tables(opened)

    late = jnp.concatenate([late, packed_b[1]], axis=0)
    late, wa0, opened = lax.optimization_barrier((late, wa0, opened))
    late = lax.all_gather(late, "shard", axis=0)

    saved0 = inner(opened, wa0, masks)
    own, moved = scatter_rep(*outer(saved0[3], saved0[4], wb0, 0))
    hat0, scale0 = hat, scale
    current = current + total_of(own, moved) + saved0[6][4:5] + saved0[6][5:6]
    hat, scale = standardize(current)
    saved1 = inner(gather_rep(hat.astype(BF)), late, masks)

    def input_grad_of(dy, hat, scale, total):
        shared = jnp.mean(total, axis=-1, keepdims=True)
        along = jnp.mean(total * hat, axis=-1, keepdims=True)
        return dy + scale * (total - shared - hat * along)

    shares, e = grad_out_of(saved1[3], saved1[4], opened, 1)
    raw_b1 = exchange_shard(shares)
    near, far, *grads = backward(e, saved1, late, late, 4, masks)
    own, moved = scatter_rep(near, far)
    grad_y = input_grad_of(grad_y, hat, scale, total_of(own, moved))
    blocks = gather_rep(grad_y.astype(BF))
    grads, _ = lax.optimization_barrier((grads, blocks[1]))
    raw_a1 = exchange_shard(grad_in(saved1[0], saved1[6], *grads))
    attended, act, _ = lax.optimization_barrier((saved1[3], saved1[4], blocks[1]))
    part = outer(attended, act, late, 4)

    shares, e = grad_out_of(saved0[3], saved0[4], blocks, 0)
    near, far, *grads = backward(e, saved0, wa0, wb0, 0, masks)
    raw0 = exchange_shard(grad_all(saved0[0], saved0[6], *grads, shares))
    part, near, raw_a1, raw_b1, _ = lax.optimization_barrier((part, near, raw_a1, raw_b1, grads))
    in_own, in_moved = scatter_rep(near, far)
    out_own, out_moved = scatter_rep(*part)
    sum_a1, sum_b1 = add_up(raw_a1), add_up(raw_b1)
    early = jnp.concatenate([sum_a1, sum_b1[:UNIT]], axis=0)
    early = in_y_order([early] + [fetch_y(early, k) for k in (1, 2, 3)], y)
    early = (early, flip_core(early))
    grad_qkv, grad_up, grad_down = unpack_early(place, *early)
    raw0, out_moved, in_moved = lax.optimization_barrier((raw0, out_moved, in_moved))
    sum0 = add_up(raw0)
    grad_y = input_grad_of(grad_y, hat0, scale0, total_of(in_own, in_moved))
    output = (current + total_of(out_own, out_moved) + saved1[6][4:5] + saved1[6][5:6]).astype(BF)
    moved = jnp.concatenate([sum_b1[UNIT:], sum0[64 + UNIT :]], axis=0)
    moved = lax.ppermute(moved, ("rep", "shard"), DENSE_OUT)
    ending = jnp.concatenate([sum0[: 64 + UNIT], moved], axis=0)
    ending = along_y(jnp.broadcast_to(ending[None], (4, TOK, D)))
    ending, grad_qkv, grad_up, grad_down = lax.optimization_barrier((ending, grad_qkv, grad_up, grad_down))
    ending = (ending, flip_core(ending))
    grad_qkv, grad_up, grad_down, grad_dense = unpack_late(place, *ending, grad_qkv, grad_up, grad_down)

    pieces = (ending, early)
    sides = [in_order(p[0][:, :47, A_LANES:], p[1][:, :47, A_LANES:], c).astype(F32) for p in pieces]
    side = jnp.stack(sides)
    sums = jnp.sum(side[:, :, :32], axis=1)
    sums = jnp.concatenate([sums, side[:, 0, 32:40]], axis=1).reshape(LAYERS, 5, D)
    sums = lax.dynamic_slice_in_dim(sums, 64 * s, 64, 2)
    grad_gains = jnp.stack([sums[:, 0], sums[:, 2]], axis=1)
    grad_shifts = jnp.stack([sums[:, 1], sums[:, 3], sums[:, 4], sums[:, 4]], axis=1)
    qkv_b = jnp.swapaxes(side[:, :, 40:43], 1, 2).reshape(LAYERS, 3 * D)
    grad_qkv_bias = lax.dynamic_slice_in_dim(qkv_b, 192 * s, 192, 1)
    up_b = side[:, :, 43:].reshape(LAYERS, REPS, FF_R)
    grad_up_bias = lax.dynamic_slice_in_dim(up_b, UNIT * s, UNIT, 2).reshape(LAYERS, 256)
    return (
        output,
        grad_y,
        grad_gains,
        grad_shifts,
        grad_qkv,
        grad_qkv_bias,
        grad_dense,
        grad_up,
        grad_up_bias,
        grad_down,
    )


def solution(mesh):
    return jax.shard_map(
        per_device,
        mesh=mesh,
        in_specs=(
            P(("rep", "shard"), None),
            P(("rep", "shard")),
            P(("rep", "shard"), None),
            P(None, None, "shard"),
            P(None, None, "shard"),
            P(None, "shard", None),
            P(None, "shard"),
            P(None, "shard", None),
            P(None, "shard", None),
            P(None, "shard"),
            P(None, "shard", None),
        ),
        out_specs=(
            P(("rep", "shard"), None),
            P(("rep", "shard"), None),
            P(None, None, "shard"),
            P(None, None, "shard"),
            P(None, "shard", None),
            P(None, "shard"),
            P(None, "shard", None),
            P(None, "shard", None),
            P(None, "shard"),
            P(None, "shard", None),
        ),
        check_vma=False,
    )
```

```python
import math

import jax
import jax.numpy as jnp
import numpy as np
from jax import lax
from jax.experimental import pallas as pl
from jax.experimental.pallas import tpu as pltpu
from jax.sharding import PartitionSpec as P

HEADS = 16
HEAD_DIM = 64
ROT = 16
LAYERS = 2
D = 1024
FF = 4096
TOK = 128
REPS = 8
SHARDS = 16
ROWS = REPS * TOK
QKV_R = 3 * D // REPS
FF_R = FF // REPS
A_LANES = QKV_R + FF_R
UNIT = FF // SHARDS // REPS
STEP = 256
EPS = 1e-05
LARGE = 58 * 2**20
SMALL = 24 * 2**20

BF = jnp.bfloat16
F32 = jnp.float32


def take_y(k):
    return [(((y + k) % 4) * 2 + c, y * 2 + c) for y in range(4) for c in range(2)]


CORE_FLIP = [(y * 2 + 1 - c, y * 2 + c) for y in range(4) for c in range(2)]


def fetch_y(a, k):
    return lax.ppermute(a, "rep", take_y(k % 4))


def flip_core(a):
    return lax.ppermute(a, "rep", CORE_FLIP)


Y_GROUPS = [[0, 2, 4, 6], [1, 3, 5, 7]]


def along_y(a):
    return lax.all_to_all(a, "rep", 0, 0, axis_index_groups=Y_GROUPS, tiled=True)


def gather_rep(block):
    near = [block] + [fetch_y(block, k) for k in (1, 2, 3)]
    return near + [flip_core(piece) for piece in near]


def in_y_order(pieces, y):
    near = jnp.zeros((4,) + pieces[0].shape, pieces[0].dtype)
    for k in range(4):
        near = lax.dynamic_update_slice_in_dim(near, pieces[k][None], (y + k) % 4, 0)
    return near


def scatter_rep(near, far):
    own, *sent = join(near, flip_core(far))
    return own, [fetch_y(sent[k - 1], -k) for k in (1, 2, 3)]


def total_of(own, moved):
    for piece in moved:
        own = own + piece.astype(F32)
    return own


def exchange_shard(a):
    return lax.all_to_all(a, "shard", 0, 0, tiled=True)


def add_up(pieces):
    return jnp.sum(pieces.astype(F32), axis=0).astype(BF)


DENSE_IN = [((s % 8) * 16 + 2 * r + s // 8, r * 16 + s) for r in range(REPS) for s in range(SHARDS)]
DENSE_OUT = [((s // 2) * 16 + 8 * (s % 2) + r, r * 16 + s) for r in range(REPS) for s in range(SHARDS)]


def dot(a, b):
    return lax.dot_general(a, b, (((1,), (0,)), ((), ())), preferred_element_type=F32)


def dot_nt(a, b):
    return lax.dot_general(a, b, (((1,), (1,)), ((), ())), preferred_element_type=F32)


def dot_tn(a, b):
    return lax.dot_general(a, b, (((0,), (0,)), ((), ())), preferred_element_type=F32)


def params(limit=SMALL):
    return pltpu.CompilerParams(vmem_limit_bytes=limit)


VMEM = pl.BlockSpec(memory_space=pltpu.VMEM)
SMEM = pl.BlockSpec(memory_space=pltpu.SMEM)


def pack_kernel(place_ref, *refs):
    qkv_refs, up_refs, (down_ref, gains_ref, moves_ref, qkv_bias_ref, up_bias_ref, first_ref, a1_ref, b_ref, a_ref) = refs[:3], refs[3:19], refs[19:]
    r, s = place_ref[0], place_ref[1]
    lane = lax.broadcasted_iota(jnp.int32, (64, 128), 1)
    row = lax.broadcasted_iota(jnp.int32, (64, 128), 0)
    for layer in range(LAYERS):
        for part in range(3):
            a_ref[layer, :, part * 128 : (part + 1) * 128] = qkv_refs[part][layer]
        for group in range(4):
            merged = jnp.zeros((64, 128), F32)
            for sub in range(4):
                piece = up_refs[4 * group + sub][layer].astype(F32)
                turned = pltpu.roll(piece, (32 * sub + 128 - 32 * (r % 4)) % 128, 1)
                merged = jnp.where(lane // 32 == sub, turned, merged)
            low = QKV_R + group * 128
            a_ref[layer, :, low : low + 128] = merged.astype(BF)
        b_ref[layer] = down_ref[layer]
        gains, moves = gains_ref[layer].astype(F32), moves_ref[layer].astype(F32)
        bias = qkv_bias_ref[layer : layer + 1].astype(F32)
        side = jnp.zeros((64, 128), F32)
        for vector, values in enumerate((gains[0:1], moves[0:1], gains[1:2], moves[1:2], moves[2:3], moves[3:4])):
            here = (row == 8 * vector + s // 2) & (lane // 64 == s % 2)
            side = jnp.where(here, jnp.concatenate([values, values], axis=1), side)
        for third in range(3):
            block = 3 * s + third
            target = jnp.where((block // 2) % 8 == r, 48 + block // 16, -1)
            here = (row == target) & (lane // 64 == block % 2)
            values = bias[:, 64 * third : 64 * (third + 1)]
            side = jnp.where(here, jnp.concatenate([values, values], axis=1), side)
        bias = up_bias_ref[layer : layer + 1].astype(F32)
        piece = jnp.where(r // 4 == 0, bias[:, :128], bias[:, 128:])
        turned = pltpu.roll(jnp.broadcast_to(piece, (64, 128)), (32 * (s % 4) + 128 - 32 * (r % 4)) % 128, 1)
        side = jnp.where((row == 51 + s // 4) & (lane // 32 == s % 4), turned, side)
        a_ref[layer, :, A_LANES:] = side.astype(BF)
    first_ref[...] = jnp.broadcast_to(a_ref[0][None], (SHARDS, 64, D))
    a1_ref[...] = a_ref[1]


def pack(place, qkv_weight, up_weight, down_weight, *vectors):
    def lanes(at):
        return pl.BlockSpec((LAYERS, 64, 128), lambda i, place: (0, 0, at(place[0])))

    def whole(a):
        return pl.BlockSpec(a.shape, lambda i, place: (0,) * a.ndim)

    return pl.pallas_call(
        pack_kernel,
        grid_spec=pltpu.PrefetchScalarGridSpec(
            num_scalar_prefetch=1,
            grid=(1,),
            in_specs=[lanes(lambda r, p=p: 8 * p + r) for p in range(3)]
            + [lanes(lambda r, o=o: 2 * o + r // 4) for o in range(16)]
            + [pl.BlockSpec((LAYERS, UNIT, D), lambda i, place: (0, place[0], 0))]
            + [whole(a) for a in vectors],
            out_specs=[
                pl.BlockSpec((SHARDS, 64, D), lambda i, place: (0, 0, 0)),
                pl.BlockSpec((64, D), lambda i, place: (0, 0)),
                pl.BlockSpec((LAYERS, UNIT, D), lambda i, place: (0, 0, 0)),
            ],
            scratch_shapes=[pltpu.VMEM((LAYERS, 64, D), BF)],
        ),
        out_shape=[
            jax.ShapeDtypeStruct((SHARDS, 64, D), BF),
            jax.ShapeDtypeStruct((64, D), BF),
            jax.ShapeDtypeStruct((LAYERS, UNIT, D), BF),
        ],
        compiler_params=params(LARGE),
        name="pack",
    )(place, *[qkv_weight] * 3, *[up_weight] * 16, down_weight, *vectors)


def put_inside(piece, r, qkv_ref, layer):
    for part in range(3):
        low = part * D + 128 * r
        qkv_ref[layer, :, low : low + 128] = piece[:, part * 128 : (part + 1) * 128]


def put_up(whole, up_ref, layer):
    lane = lax.broadcasted_iota(jnp.int32, (64, 128), 1)
    for s in range(SHARDS):
        group, sub = s // 4, s % 4
        for half in range(2):
            merged = jnp.zeros((64, 128), F32)
            for inner_r in range(4):
                piece = whole[4 * half + inner_r][:, group * 128 : (group + 1) * 128]
                shift = (32 * inner_r - 32 * sub) % 128
                turned = pltpu.roll(piece, shift, 1) if shift else piece
                merged = jnp.where(lane // 32 == inner_r, turned, merged)
            low = 256 * s + 128 * half
            up_ref[layer, :, low : low + 128] = merged


def put_layer(place_ref, near_ref, far_ref, qkv_ref, up_ref, down_ref, dense_ref=None):
    c = place_ref[0] % 2
    whole = []
    for r in range(REPS):
        piece = jnp.where(c == r % 2, near_ref[r // 2], far_ref[r // 2]).astype(F32)
        put_inside(piece[:64], r, qkv_ref, 0)
        whole.append(piece[:64, QKV_R:A_LANES])
        down_ref[0, UNIT * r : UNIT * (r + 1), :] = piece[64:96]
        if dense_ref is not None:
            dense_ref[1, 8 * r : 8 * r + 8, :] = piece[96:104]
            dense_ref[0, 8 * r : 8 * r + 8, :] = piece[112:120]
    put_up(whole, up_ref, 0)


def unpack_late_kernel(place_ref, near_ref, far_ref, qkv_in, up_in, down_in, *out_refs):
    put_layer(place_ref, near_ref, far_ref, *out_refs)


UNPACKED = [
    jax.ShapeDtypeStruct((LAYERS, 64, 3 * D), F32),
    jax.ShapeDtypeStruct((LAYERS, 64, FF), F32),
    jax.ShapeDtypeStruct((LAYERS, 256, D), F32),
]


def layer_specs(layer):
    return [pl.BlockSpec((1,) + a.shape[1:], lambda i: (layer, 0, 0)) for a in UNPACKED]


def unpack_early(place, near, far):
    return pl.pallas_call(
        put_layer,
        grid=(1,),
        in_specs=[SMEM, VMEM, VMEM],
        out_specs=layer_specs(1),
        out_shape=UNPACKED,
        compiler_params=params(),
        name="unpack_early",
    )(place, near, far)


def unpack_late(place, near, far, *filled):
    return pl.pallas_call(
        unpack_late_kernel,
        grid=(1,),
        in_specs=[SMEM, VMEM, VMEM] + [pl.BlockSpec(memory_space=pl.ANY)] * 3,
        out_specs=layer_specs(0) + [VMEM],
        out_shape=UNPACKED + [jax.ShapeDtypeStruct((LAYERS, 64, D), F32)],
        input_output_aliases={3: 0, 4: 1, 5: 2},
        compiler_params=params(),
        name="unpack_late",
    )(place, near, far, *filled)


def join_kernel(near_ref, far_ref, own_ref, *sent_refs):
    for k in range(4):
        rows = slice(k * TOK, (k + 1) * TOK)
        both = near_ref[rows].astype(F32) + far_ref[rows].astype(F32)
        if k == 0:
            own_ref[...] = both
        else:
            sent_refs[k - 1][...] = both.astype(BF)


def join(near, far):
    sent = jax.ShapeDtypeStruct((TOK, D), BF)
    return pl.pallas_call(
        join_kernel,
        in_specs=[VMEM, VMEM],
        out_specs=[VMEM] * 4,
        out_shape=[jax.ShapeDtypeStruct((TOK, D), F32), sent, sent, sent],
        compiler_params=params(),
        name="join",
    )(near, far)


def rotary_table():
    angle = np.arange(TOK, dtype=np.float64)[:, None] * (10000.0 ** (-2.0 * np.arange(8) / ROT))[None, :]
    lane = np.arange(128) % HEAD_DIM
    cos_n = np.where(lane[None, :] < ROT, np.cos(angle)[:, lane % 8], 1.0)
    low_n = np.where(lane[None, :] < 8, -np.sin(angle)[:, lane % 8], 0.0)
    high_n = np.where((lane[None, :] >= 8) & (lane[None, :] < ROT), np.sin(angle)[:, lane % 8], 0.0)
    rest = np.concatenate([cos_n, low_n, high_n], axis=1).astype(np.float32)
    parts = []
    for _ in range(3):
        parts.append(rest.astype(BF))
        rest = rest - parts[-1].astype(np.float32)
    return np.stack(parts)


def tables_kernel(table_ref, *refs):
    pieces, (mask_ref, cos_ref, low_ref, high_ref) = refs[:REPS], refs[REPS:]
    row = lax.broadcasted_iota(jnp.int32, (TOK, TOK), 0)
    col = lax.broadcasted_iota(jnp.int32, (TOK, TOK), 1)
    for block in range(REPS):
        rows = slice(block * TOK, (block + 1) * TOK)
        docs = jnp.broadcast_to(pieces[block][...].astype(F32)[0:1], (TOK, TOK))
        mask = jnp.where((docs == docs.T) & (col <= row), 1.0, 0.0)
        mask_ref[rows] = mask
        places = jnp.sum(mask, axis=1, keepdims=True) - 1.0
        chosen = jnp.where(col.astype(F32) == places, 1.0, 0.0).astype(BF)
        found = dot(chosen, table_ref[0]) + dot(chosen, table_ref[1]) + dot(chosen, table_ref[2])
        cos_ref[rows] = found[:, :128]
        low_ref[rows] = found[:, 128:256]
        high_ref[rows] = found[:, 256:]


def token_tables(opened):
    return pl.pallas_call(
        tables_kernel,
        grid=(1,),
        in_specs=[VMEM] + [pl.BlockSpec((16, 128), lambda i: (16, 0))] * REPS,
        out_specs=[VMEM] * 4,
        out_shape=[jax.ShapeDtypeStruct((ROWS, 128), F32)] * 4,
        compiler_params=params(),
        name="tables",
    )(jnp.asarray(rotary_table()), *opened)


def turn(values, cos_t, low_t, high_t):
    return values * cos_t + pltpu.roll(values, 120, 1) * low_t + pltpu.roll(values, 8, 1) * high_t


def turn_back(values, cos_t, low_t, high_t):
    return values * cos_t - pltpu.roll(values, 120, 1) * low_t - pltpu.roll(values, 8, 1) * high_t


def row_spec(lanes):
    return pl.BlockSpec((STEP, lanes), lambda i: (i, 0))


def whole_spec(shape):
    return pl.BlockSpec(shape, lambda i: (0,) * len(shape))


PROB_SPEC = pl.BlockSpec((STEP // TOK, 2, TOK, TOK), lambda i: (i, 0, 0, 0))
WA_SPEC = whole_spec((SHARDS, 64, D))
HELD = [pltpu.VMEM((FF_R, D), BF), pltpu.VMEM((128, D), BF)]


def wb_specs(at):
    return [pl.BlockSpec((SHARDS, 16, D), lambda i, k=k: (0, at + k, 0)) for k in range(3)]


def hold_weights(wb_refs, wd_ref, wo_ref):
    @pl.when(pl.program_id(0) == 0)
    def _():
        rows = jnp.concatenate([wb_refs[0][...], wb_refs[1][...]], axis=1)
        wd_ref[...] = rows.reshape(FF_R, D)
        wo_ref[...] = wb_refs[2][...].astype(F32)[:, :8].reshape(128, D).astype(BF)


VEC_SPEC = whole_spec((16, D))
NEAR_SPEC = pl.BlockSpec((STEP, D), lambda i: (jnp.minimum(i, 1), 0))
FAR_SPEC = pl.BlockSpec((STEP, D), lambda i: (jnp.maximum(i - 2, 0), 0))


def rows_of(lanes, dtype):
    return jax.ShapeDtypeStruct((ROWS, lanes), dtype)


def put_block(near_ref, far_ref, values):
    @pl.when(pl.program_id(0) < 2)
    def _():
        near_ref[...] = values

    @pl.when(pl.program_id(0) >= 2)
    def _():
        far_ref[...] = values


def inner_kernel(*refs):
    pieces, (wa_ref, mask_ref, cos_ref, low_ref, high_ref) = refs[:REPS], refs[REPS : REPS + 5]
    xh_ref, qkv_ref, prob_ref, o_ref, act_ref, slope_ref, vec_ref = refs[REPS + 5 :]

    @pl.when(pl.program_id(0) == 0)
    def _():
        side = jnp.zeros((64, 128), F32)
        for shard in range(SHARDS):
            side = side + wa_ref[shard, :, A_LANES:].astype(F32)
        vec_ref[...] = jnp.zeros_like(vec_ref)
        for vector in range(6):
            for j in range(8):
                vec_ref[vector : vector + 1, 128 * j : 128 * (j + 1)] = side[8 * vector + j : 8 * vector + j + 1]
        for j in range(7):
            vec_ref[6:7, 128 * j : 128 * (j + 1)] = side[48 + j : 49 + j]

    for step in range(4):

        @pl.when(pl.program_id(0) == step)
        def _(step=step):
            xh_ref[:TOK] = pieces[2 * step][...]
            xh_ref[TOK:] = pieces[2 * step + 1][...]

    xh = xh_ref[...].astype(F32)
    h1 = (xh * vec_ref[0:1] + vec_ref[1:2]).astype(BF)
    h2 = (xh * vec_ref[2:3] + vec_ref[3:4]).astype(BF)
    mixed = dot(h1, wa_ref[:, :, :QKV_R].reshape(D, QKV_R)) + vec_ref[6:7, :QKV_R]
    tables = (cos_ref[...], low_ref[...], high_ref[...])
    q = turn(mixed[:, :128], *tables).astype(BF)
    k = turn(mixed[:, 128:256], *tables).astype(BF)
    v = mixed[:, 256:].astype(BF)
    qkv_ref[:, :128] = q
    qkv_ref[:, 128:256] = k
    qkv_ref[:, 256:] = v
    u = dot(h2, wa_ref[:, :, QKV_R:A_LANES].reshape(D, FF_R)) + vec_ref[6:7, QKV_R:A_LANES]
    share = 0.5 * (1.0 + lax.erf(u * math.sqrt(0.5)))
    act_ref[...] = (u * share).astype(BF)
    slope_ref[...] = share + u * jnp.exp(-0.5 * u * u) * (1.0 / math.sqrt(2.0 * math.pi))
    first = lax.broadcasted_iota(jnp.int32, (TOK, 128), 1) < HEAD_DIM
    zero = jnp.zeros((TOK, 128), BF)
    for block in range(STEP // TOK):
        rows = slice(block * TOK, (block + 1) * TOK)
        allowed = mask_ref[rows] > 0.5
        out = jnp.zeros((TOK, 128), F32)
        for head in range(2):
            mine = first if head == 0 else jnp.logical_not(first)
            scores = dot_nt(jnp.where(mine, q[rows], zero), k[rows]) * HEAD_DIM**-0.5
            scores = jnp.where(allowed, scores, -1e30)
            raised = jnp.exp(scores - jnp.max(scores, axis=-1, keepdims=True))
            prob = raised / jnp.sum(raised, axis=-1, keepdims=True)
            prob_ref[block, head] = prob
            out = out + dot(prob.astype(BF), jnp.where(mine, v[rows], zero))
        o_ref[rows] = out.astype(BF)


def inner(blocks, wa, masks):
    return pl.pallas_call(
        inner_kernel,
        grid=(ROWS // STEP,),
        in_specs=[whole_spec((TOK, D))] * REPS + [WA_SPEC] + [row_spec(128)] * 4,
        out_specs=[row_spec(D), row_spec(QKV_R), PROB_SPEC, row_spec(128), row_spec(FF_R), row_spec(FF_R), VEC_SPEC],
        out_shape=[
            rows_of(D, BF),
            rows_of(QKV_R, BF),
            jax.ShapeDtypeStruct((REPS, 2, TOK, TOK), F32),
            rows_of(128, BF),
            rows_of(FF_R, BF),
            rows_of(FF_R, F32),
            jax.ShapeDtypeStruct((16, D), F32),
        ],
        compiler_params=params(LARGE),
        name="inner",
    )(*blocks, wa, *masks)


HALF = jax.ShapeDtypeStruct((ROWS // 2, D), BF)


def outer_kernel(o_ref, act_ref, down0_ref, down1_ref, dense_ref, near_ref, far_ref, wd_ref, wo_ref):
    hold_weights((down0_ref, down1_ref, dense_ref), wd_ref, wo_ref)
    part = dot(o_ref[...], wo_ref[...]) + dot(act_ref[...], wd_ref[...])
    put_block(near_ref, far_ref, part.astype(BF))


def outer(attended, act, wb, at):
    return pl.pallas_call(
        outer_kernel,
        grid=(ROWS // STEP,),
        in_specs=[row_spec(128), row_spec(FF_R)] + wb_specs(at),
        out_specs=[NEAR_SPEC, FAR_SPEC],
        out_shape=[HALF, HALF],
        scratch_shapes=HELD,
        compiler_params=params(),
        name="outer",
    )(attended, act, wb, wb, wb)


def backward_kernel(
    e_ref, xh_ref, qkv_ref, prob_ref, slope_ref, wa_ref, down0_ref, down1_ref, dense_ref, vec_ref, cos_ref, low_ref, high_ref,
    near_ref, far_ref, dc_ref, du_ref, side_ref, wd_ref, wo_ref,
):
    def add_row(at, values):
        for j in range(values.shape[1] // 128):
            side_ref[at + j : at + j + 1] += values[:, 128 * j : 128 * (j + 1)]

    @pl.when(pl.program_id(0) == 0)
    def _():
        side_ref[...] = jnp.zeros_like(side_ref)

    hold_weights((down0_ref, down1_ref, dense_ref), wd_ref, wo_ref)
    e = e_ref[...]
    add_row(32, jnp.sum(e.astype(F32), axis=0, keepdims=True))
    du = (dot_nt(e, wd_ref[...]) * slope_ref[...]).astype(BF)
    du_ref[...] = du
    grad_o = dot_nt(e, wo_ref[...]).astype(BF)
    tables = (cos_ref[...], low_ref[...], high_ref[...])
    first = lax.broadcasted_iota(jnp.int32, (TOK, 128), 1) < HEAD_DIM
    zero = jnp.zeros((TOK, 128), BF)
    grads = ([], [], [])
    for block in range(STEP // TOK):
        rows = slice(block * TOK, (block + 1) * TOK)
        q, k, v = qkv_ref[rows, :128], qkv_ref[rows, 128:256], qkv_ref[rows, 256:]
        dq = jnp.zeros((TOK, 128), F32)
        dk = jnp.zeros((TOK, 128), F32)
        dv = jnp.zeros((TOK, 128), F32)
        for head in range(2):
            mine = first if head == 0 else jnp.logical_not(first)
            prob = prob_ref[block, head]
            grad_head = jnp.where(mine, grad_o[rows], zero)
            dv = dv + dot_tn(prob.astype(BF), grad_head)
            grad_prob = dot_nt(grad_head, v)
            inner_sum = jnp.sum(prob * grad_prob, axis=-1, keepdims=True)
            ds = (prob * (grad_prob - inner_sum)).astype(BF)
            dq = dq + dot(ds, jnp.where(mine, k, zero))
            dk = dk + dot_tn(ds, jnp.where(mine, q, zero))
        grads[0].append(dq * HEAD_DIM**-0.5)
        grads[1].append(dk * HEAD_DIM**-0.5)
        grads[2].append(dv)
    dq, dk, dv = (jnp.concatenate(g, axis=0) for g in grads)
    dc = jnp.concatenate([turn_back(dq, *tables), turn_back(dk, *tables), dv], axis=1).astype(BF)
    dc_ref[...] = dc
    dh1 = dot_nt(dc, wa_ref[:, :, :QKV_R].reshape(D, QKV_R))
    dh2 = dot_nt(du, wa_ref[:, :, QKV_R:A_LANES].reshape(D, FF_R))
    put_block(near_ref, far_ref, (dh1 * vec_ref[0:1] + dh2 * vec_ref[2:3]).astype(BF))
    xh = xh_ref[...].astype(F32)
    add_row(0, jnp.sum(dh1 * xh, axis=0, keepdims=True))
    add_row(8, jnp.sum(dh1, axis=0, keepdims=True))
    add_row(16, jnp.sum(dh2 * xh, axis=0, keepdims=True))
    add_row(24, jnp.sum(dh2, axis=0, keepdims=True))
    add_row(40, jnp.sum(dc.astype(F32), axis=0, keepdims=True))
    add_row(43, jnp.sum(du.astype(F32), axis=0, keepdims=True))


def backward(e, kept, wa, wb, at, masks):
    xh, qkv, prob, _, _, slope, vectors = kept
    return pl.pallas_call(
        backward_kernel,
        grid=(ROWS // STEP,),
        in_specs=[row_spec(D), row_spec(D), row_spec(QKV_R), PROB_SPEC, row_spec(FF_R)]
        + [WA_SPEC]
        + wb_specs(at)
        + [VEC_SPEC]
        + [row_spec(128)] * 3,
        out_specs=[NEAR_SPEC, FAR_SPEC, row_spec(QKV_R), row_spec(FF_R), whole_spec((64, 128))],
        out_shape=[
            HALF,
            HALF,
            rows_of(QKV_R, BF),
            rows_of(FF_R, BF),
            jax.ShapeDtypeStruct((64, 128), F32),
        ],
        scratch_shapes=HELD,
        compiler_params=params(LARGE),
        name="backward",
    )(e, xh, qkv, prob, slope, wa, wb, wb, wb, vectors, *masks[1:])


def grad_in_kernel(xh_ref, vec_ref, dc_ref, du_ref, side_ref, out_ref):
    xh = xh_ref[...].astype(F32)
    h1 = (xh * vec_ref[0:1] + vec_ref[1:2]).astype(BF)
    h2 = (xh * vec_ref[2:3] + vec_ref[3:4]).astype(BF)
    out_ref[:, :, :QKV_R] = dot_tn(h1, dc_ref[...]).astype(BF).reshape(4, 64, QKV_R)
    out_ref[:, :, QKV_R:A_LANES] = dot_tn(h2, du_ref[...]).astype(BF).reshape(4, 64, FF_R)
    out_ref[:, :, A_LANES:] = jnp.broadcast_to(side_ref[...].astype(BF)[None], (4, 64, 128))


def grad_all_kernel(xh_ref, vec_ref, dc_ref, du_ref, side_ref, shares_ref, out_ref):
    grad_in_kernel(xh_ref, vec_ref, dc_ref, du_ref, side_ref, out_ref.at[:, :64])
    out_ref[:, 64:] = shares_ref[...]


def grad_all(xh, vectors, dc, du, side, shares):
    return pl.pallas_call(
        grad_all_kernel,
        grid=(4,),
        in_specs=[
            pl.BlockSpec((ROWS, 256), lambda i: (0, i)),
            pl.BlockSpec((16, 256), lambda i: (0, i)),
            whole_spec((ROWS, QKV_R)),
            whole_spec((ROWS, FF_R)),
            whole_spec((64, 128)),
            pl.BlockSpec((4, 48, D), lambda i: (i, 0, 0)),
        ],
        out_specs=pl.BlockSpec((4, 112, D), lambda i: (i, 0, 0)),
        out_shape=jax.ShapeDtypeStruct((SHARDS, 112, D), BF),
        compiler_params=params(),
        name="grad_all",
    )(xh, vectors, dc, du, side, shares)


def grad_in(xh, vectors, dc, du, side):
    return pl.pallas_call(
        grad_in_kernel,
        grid=(4,),
        in_specs=[
            pl.BlockSpec((ROWS, 256), lambda i: (0, i)),
            pl.BlockSpec((16, 256), lambda i: (0, i)),
            whole_spec((ROWS, QKV_R)),
            whole_spec((ROWS, FF_R)),
            whole_spec((64, 128)),
        ],
        out_specs=pl.BlockSpec((4, 64, D), lambda i: (i, 0, 0)),
        out_shape=jax.ShapeDtypeStruct((SHARDS, 64, D), BF),
        compiler_params=params(),
        name="grad_in",
    )(xh, vectors, dc, du, side)


def grad_out_kernel(o_ref, act_ref, *refs):
    pieces, (out_ref, e_ref) = refs[:REPS], refs[REPS:]
    e = jnp.concatenate([piece[...] for piece in pieces], axis=0)
    e_ref[...] = e
    down = dot_tn(act_ref[...], e).reshape(SHARDS, UNIT, 256)
    dense = dot_tn(o_ref[...], e).reshape(SHARDS, 8, 256)
    empty = jnp.zeros((SHARDS, 8, 256), F32)
    out_ref[...] = jnp.concatenate([down, dense, empty], axis=1).astype(BF)


def grad_out_of(attended, act, blocks, at):
    return pl.pallas_call(
        grad_out_kernel,
        grid=(4,),
        in_specs=[
            whole_spec((ROWS, 128)),
            whole_spec((ROWS, FF_R)),
        ]
        + [pl.BlockSpec((TOK, 256), lambda i: (at, i))] * REPS,
        out_specs=[
            pl.BlockSpec((SHARDS, 48, 256), lambda i: (0, 0, i)),
            pl.BlockSpec((ROWS, 256), lambda i: (0, i)),
        ],
        out_shape=[jax.ShapeDtypeStruct((SHARDS, 48, D), BF), rows_of(D, BF)],
        compiler_params=params(),
        name="grad_out",
    )(attended, act, *blocks)


def standardize(x):
    centered = x - jnp.mean(x, axis=-1, keepdims=True)
    scale = lax.rsqrt(jnp.mean(centered * centered, axis=-1, keepdims=True) + EPS)
    return centered * scale, scale


def in_order(near, far, c):
    return jnp.stack([jnp.where(c == 0, near, far), jnp.where(c == 0, far, near)], axis=1).reshape((REPS,) + near.shape[1:])


def per_device(
    tokens, doc_ids, grad_out, norm_gains, shifts, qkv_weight, qkv_bias, dense_weight, up_weight, up_bias, down_weight
):
    r = lax.axis_index("rep").astype(jnp.int32)
    s = lax.axis_index("shard").astype(jnp.int32)
    y, c = r // 2, r % 2
    place = jnp.stack([r, s])

    dense = lax.dynamic_slice_in_dim(dense_weight, 8 * r, 8, 1)
    dense = lax.ppermute(dense, ("rep", "shard"), DENSE_IN)
    first, late, packed_b = pack(place, qkv_weight, up_weight, down_weight, norm_gains, shifts, qkv_bias, up_bias)
    packed_b = jnp.concatenate([packed_b, dense, jnp.zeros((LAYERS, 8, D), BF)], axis=1)
    wa0 = exchange_shard(first)

    current = tokens.astype(F32)
    hat, scale = standardize(current)
    live = (doc_ids >= 0).astype(F32)[:, None]
    grad_y = grad_out.astype(F32) * live
    marks = jnp.pad(doc_ids.astype(BF).reshape(1, TOK), ((0, 15), (0, D - TOK)))
    opened = gather_rep(jnp.concatenate([hat.astype(BF), grad_y.astype(BF), marks], axis=0))
    masks = token_tables(opened)

    late = jnp.concatenate([late, packed_b[1]], axis=0)
    late, lower, wa0, opened = lax.optimization_barrier((late, packed_b[0], wa0, opened))
    wb0 = exchange_shard(jnp.broadcast_to(lower[None], (SHARDS, 48, D)))
    late = lax.all_gather(late, "shard", axis=0)

    saved0 = inner(opened, wa0, masks)
    own, moved = scatter_rep(*outer(saved0[3], saved0[4], wb0, 0))
    hat0, scale0 = hat, scale
    current = current + total_of(own, moved) + saved0[6][4:5] + saved0[6][5:6]
    hat, scale = standardize(current)
    saved1 = inner(gather_rep(hat.astype(BF)), late, masks)

    def input_grad_of(dy, hat, scale, total):
        shared = jnp.mean(total, axis=-1, keepdims=True)
        along = jnp.mean(total * hat, axis=-1, keepdims=True)
        return dy + scale * (total - shared - hat * along)

    shares, e = grad_out_of(saved1[3], saved1[4], opened, 1)
    raw_b1 = exchange_shard(shares)
    near, far, *grads = backward(e, saved1, late, late, 4, masks)
    own, moved = scatter_rep(near, far)
    grad_y = input_grad_of(grad_y, hat, scale, total_of(own, moved))
    blocks = gather_rep(grad_y.astype(BF))
    grads, _ = lax.optimization_barrier((grads, blocks[1]))
    raw_a1 = exchange_shard(grad_in(saved1[0], saved1[6], *grads))
    attended, act, _ = lax.optimization_barrier((saved1[3], saved1[4], blocks[1]))
    part = outer(attended, act, late, 4)

    shares, e = grad_out_of(saved0[3], saved0[4], blocks, 0)
    near, far, *grads = backward(e, saved0, wa0, wb0, 0, masks)
    raw0 = exchange_shard(grad_all(saved0[0], saved0[6], *grads, shares))
    part, near, raw_a1, raw_b1, _ = lax.optimization_barrier((part, near, raw_a1, raw_b1, grads))
    in_own, in_moved = scatter_rep(near, far)
    out_own, out_moved = scatter_rep(*part)
    sum_a1, sum_b1 = add_up(raw_a1), add_up(raw_b1)
    early = jnp.concatenate([sum_a1, sum_b1[:UNIT]], axis=0)
    early = in_y_order([early] + [fetch_y(early, k) for k in (1, 2, 3)], y)
    early = (early, flip_core(early))
    grad_qkv, grad_up, grad_down = unpack_early(place, *early)
    raw0, out_moved, in_moved = lax.optimization_barrier((raw0, out_moved, in_moved))
    sum0 = add_up(raw0)
    grad_y = input_grad_of(grad_y, hat0, scale0, total_of(in_own, in_moved))
    output = (current + total_of(out_own, out_moved) + saved1[6][4:5] + saved1[6][5:6]).astype(BF)
    moved = jnp.concatenate([sum_b1[UNIT:], sum0[64 + UNIT :]], axis=0)
    moved = lax.ppermute(moved, ("rep", "shard"), DENSE_OUT)
    ending = jnp.concatenate([sum0[: 64 + UNIT], moved], axis=0)
    ending = along_y(jnp.broadcast_to(ending[None], (4, TOK, D)))
    ending, grad_qkv, grad_up, grad_down = lax.optimization_barrier((ending, grad_qkv, grad_up, grad_down))
    ending = (ending, flip_core(ending))
    grad_qkv, grad_up, grad_down, grad_dense = unpack_late(place, *ending, grad_qkv, grad_up, grad_down)

    pieces = (ending, early)
    sides = [in_order(p[0][:, :47, A_LANES:], p[1][:, :47, A_LANES:], c).astype(F32) for p in pieces]
    side = jnp.stack(sides)
    sums = jnp.sum(side[:, :, :32], axis=1)
    sums = jnp.concatenate([sums, side[:, 0, 32:40]], axis=1).reshape(LAYERS, 5, D)
    sums = lax.dynamic_slice_in_dim(sums, 64 * s, 64, 2)
    grad_gains = jnp.stack([sums[:, 0], sums[:, 2]], axis=1)
    grad_shifts = jnp.stack([sums[:, 1], sums[:, 3], sums[:, 4], sums[:, 4]], axis=1)
    qkv_b = jnp.swapaxes(side[:, :, 40:43], 1, 2).reshape(LAYERS, 3 * D)
    grad_qkv_bias = lax.dynamic_slice_in_dim(qkv_b, 192 * s, 192, 1)
    up_b = side[:, :, 43:].reshape(LAYERS, REPS, FF_R)
    grad_up_bias = lax.dynamic_slice_in_dim(up_b, UNIT * s, UNIT, 2).reshape(LAYERS, 256)
    return (
        output,
        grad_y,
        grad_gains,
        grad_shifts,
        grad_qkv,
        grad_qkv_bias,
        grad_dense,
        grad_up,
        grad_up_bias,
        grad_down,
    )


def solution(mesh):
    return jax.shard_map(
        per_device,
        mesh=mesh,
        in_specs=(
            P(("rep", "shard"), None),
            P(("rep", "shard")),
            P(("rep", "shard"), None),
            P(None, None, "shard"),
            P(None, None, "shard"),
            P(None, "shard", None),
            P(None, "shard"),
            P(None, "shard", None),
            P(None, "shard", None),
            P(None, "shard"),
            P(None, "shard", None),
        ),
        out_specs=(
            P(("rep", "shard"), None),
            P(("rep", "shard"), None),
            P(None, None, "shard"),
            P(None, None, "shard"),
            P(None, "shard", None),
            P(None, "shard"),
            P(None, "shard", None),
            P(None, "shard", None),
            P(None, "shard"),
            P(None, "shard", None),
        ),
        check_vma=False,
    )
```

```python
import math

import jax
import jax.numpy as jnp
import numpy as np
from jax import lax
from jax.experimental import pallas as pl
from jax.experimental.pallas import tpu as pltpu
from jax.sharding import PartitionSpec as P

HEADS = 16
HEAD_DIM = 64
ROT = 16
LAYERS = 2
D = 1024
FF = 4096
TOK = 128
REPS = 8
SHARDS = 16
ROWS = REPS * TOK
QKV_R = 3 * D // REPS
FF_R = FF // REPS
A_LANES = QKV_R + FF_R
UNIT = FF // SHARDS // REPS
STEP = 256
EPS = 1e-05
LARGE = 58 * 2**20
SMALL = 24 * 2**20

BF = jnp.bfloat16
F32 = jnp.float32


def take_y(k):
    return [(((y + k) % 4) * 2 + c, y * 2 + c) for y in range(4) for c in range(2)]


CORE_FLIP = [(y * 2 + 1 - c, y * 2 + c) for y in range(4) for c in range(2)]


def fetch_y(a, k):
    return lax.ppermute(a, "rep", take_y(k % 4))


def flip_core(a):
    return lax.ppermute(a, "rep", CORE_FLIP)


Y_GROUPS = [[0, 2, 4, 6], [1, 3, 5, 7]]


def along_y(a):
    return lax.all_to_all(a, "rep", 0, 0, axis_index_groups=Y_GROUPS, tiled=True)


def gather_rep(block):
    near = [block] + [fetch_y(block, k) for k in (1, 2, 3)]
    return near + [flip_core(piece) for piece in near]


def in_y_order(pieces, y):
    near = jnp.zeros((4,) + pieces[0].shape, pieces[0].dtype)
    for k in range(4):
        near = lax.dynamic_update_slice_in_dim(near, pieces[k][None], (y + k) % 4, 0)
    return near


def scatter_rep(near, far):
    own, *sent = join(near, flip_core(far))
    return own, [fetch_y(sent[k - 1], -k) for k in (1, 2, 3)]


def total_of(own, moved):
    for piece in moved:
        own = own + piece.astype(F32)
    return own


def exchange_shard(a):
    return lax.all_to_all(a, "shard", 0, 0, tiled=True)


def add_up(pieces):
    return jnp.sum(pieces.astype(F32), axis=0).astype(BF)


DENSE_IN = [((s % 8) * 16 + 2 * r + s // 8, r * 16 + s) for r in range(REPS) for s in range(SHARDS)]
DENSE_OUT = [((s // 2) * 16 + 8 * (s % 2) + r, r * 16 + s) for r in range(REPS) for s in range(SHARDS)]


def dot(a, b):
    return lax.dot_general(a, b, (((1,), (0,)), ((), ())), preferred_element_type=F32)


def dot_nt(a, b):
    return lax.dot_general(a, b, (((1,), (1,)), ((), ())), preferred_element_type=F32)


def dot_tn(a, b):
    return lax.dot_general(a, b, (((0,), (0,)), ((), ())), preferred_element_type=F32)


def params(limit=SMALL):
    return pltpu.CompilerParams(vmem_limit_bytes=limit)


VMEM = pl.BlockSpec(memory_space=pltpu.VMEM)
SMEM = pl.BlockSpec(memory_space=pltpu.SMEM)


def pack_kernel(place_ref, *refs):
    qkv_refs, up_refs, (down_ref, gains_ref, moves_ref, qkv_bias_ref, up_bias_ref, first_ref, a1_ref, b_ref, a_ref) = refs[:3], refs[3:19], refs[19:]
    r, s = place_ref[0], place_ref[1]
    lane = lax.broadcasted_iota(jnp.int32, (64, 128), 1)
    row = lax.broadcasted_iota(jnp.int32, (64, 128), 0)
    for layer in range(LAYERS):
        for part in range(3):
            a_ref[layer, :, part * 128 : (part + 1) * 128] = qkv_refs[part][layer]
        for group in range(4):
            merged = jnp.zeros((64, 128), F32)
            for sub in range(4):
                piece = up_refs[4 * group + sub][layer].astype(F32)
                turned = pltpu.roll(piece, (32 * sub + 128 - 32 * (r % 4)) % 128, 1)
                merged = jnp.where(lane // 32 == sub, turned, merged)
            low = QKV_R + group * 128
            a_ref[layer, :, low : low + 128] = merged.astype(BF)
        b_ref[layer] = down_ref[layer]
        gains, moves = gains_ref[layer].astype(F32), moves_ref[layer].astype(F32)
        bias = qkv_bias_ref[layer : layer + 1].astype(F32)
        side = jnp.zeros((64, 128), F32)
        for vector, values in enumerate((gains[0:1], moves[0:1], gains[1:2], moves[1:2], moves[2:3], moves[3:4])):
            here = (row == 8 * vector + s // 2) & (lane // 64 == s % 2)
            side = jnp.where(here, jnp.concatenate([values, values], axis=1), side)
        for third in range(3):
            block = 3 * s + third
            target = jnp.where((block // 2) % 8 == r, 48 + block // 16, -1)
            here = (row == target) & (lane // 64 == block % 2)
            values = bias[:, 64 * third : 64 * (third + 1)]
            side = jnp.where(here, jnp.concatenate([values, values], axis=1), side)
        bias = up_bias_ref[layer : layer + 1].astype(F32)
        piece = jnp.where(r // 4 == 0, bias[:, :128], bias[:, 128:])
        turned = pltpu.roll(jnp.broadcast_to(piece, (64, 128)), (32 * (s % 4) + 128 - 32 * (r % 4)) % 128, 1)
        side = jnp.where((row == 51 + s // 4) & (lane // 32 == s % 4), turned, side)
        a_ref[layer, :, A_LANES:] = side.astype(BF)
    first_ref[...] = jnp.broadcast_to(a_ref[0][None], (SHARDS, 64, D))
    a1_ref[...] = a_ref[1]


def pack(place, qkv_weight, up_weight, down_weight, *vectors):
    def lanes(at):
        return pl.BlockSpec((LAYERS, 64, 128), lambda i, place: (0, 0, at(place[0])))

    def whole(a):
        return pl.BlockSpec(a.shape, lambda i, place: (0,) * a.ndim)

    return pl.pallas_call(
        pack_kernel,
        grid_spec=pltpu.PrefetchScalarGridSpec(
            num_scalar_prefetch=1,
            grid=(1,),
            in_specs=[lanes(lambda r, p=p: 8 * p + r) for p in range(3)]
            + [lanes(lambda r, o=o: 2 * o + r // 4) for o in range(16)]
            + [pl.BlockSpec((LAYERS, UNIT, D), lambda i, place: (0, place[0], 0))]
            + [whole(a) for a in vectors],
            out_specs=[
                pl.BlockSpec((SHARDS, 64, D), lambda i, place: (0, 0, 0)),
                pl.BlockSpec((64, D), lambda i, place: (0, 0)),
                pl.BlockSpec((LAYERS, UNIT, D), lambda i, place: (0, 0, 0)),
            ],
            scratch_shapes=[pltpu.VMEM((LAYERS, 64, D), BF)],
        ),
        out_shape=[
            jax.ShapeDtypeStruct((SHARDS, 64, D), BF),
            jax.ShapeDtypeStruct((64, D), BF),
            jax.ShapeDtypeStruct((LAYERS, UNIT, D), BF),
        ],
        compiler_params=params(LARGE),
        name="pack",
    )(place, *[qkv_weight] * 3, *[up_weight] * 16, down_weight, *vectors)


def put_inside(piece, r, qkv_ref, layer):
    for part in range(3):
        low = part * D + 128 * r
        qkv_ref[layer, :, low : low + 128] = piece[:, part * 128 : (part + 1) * 128]


def put_up(whole, up_ref, layer):
    lane = lax.broadcasted_iota(jnp.int32, (64, 128), 1)
    for s in range(SHARDS):
        group, sub = s // 4, s % 4
        for half in range(2):
            merged = jnp.zeros((64, 128), F32)
            for inner_r in range(4):
                piece = whole[4 * half + inner_r][:, group * 128 : (group + 1) * 128]
                shift = (32 * inner_r - 32 * sub) % 128
                turned = pltpu.roll(piece, shift, 1) if shift else piece
                merged = jnp.where(lane // 32 == inner_r, turned, merged)
            low = 256 * s + 128 * half
            up_ref[layer, :, low : low + 128] = merged


def put_layer(place_ref, near_ref, far_ref, qkv_ref, up_ref, down_ref, dense_ref=None):
    c = place_ref[0] % 2
    whole = []
    for r in range(REPS):
        piece = jnp.where(c == r % 2, near_ref[r // 2], far_ref[r // 2]).astype(F32)
        put_inside(piece[:64], r, qkv_ref, 0)
        whole.append(piece[:64, QKV_R:A_LANES])
        down_ref[0, UNIT * r : UNIT * (r + 1), :] = piece[64:96]
        if dense_ref is not None:
            dense_ref[1, 8 * r : 8 * r + 8, :] = piece[96:104]
            dense_ref[0, 8 * r : 8 * r + 8, :] = piece[112:120]
    put_up(whole, up_ref, 0)


def unpack_late_kernel(place_ref, near_ref, far_ref, qkv_in, up_in, down_in, *out_refs):
    put_layer(place_ref, near_ref, far_ref, *out_refs)


UNPACKED = [
    jax.ShapeDtypeStruct((LAYERS, 64, 3 * D), F32),
    jax.ShapeDtypeStruct((LAYERS, 64, FF), F32),
    jax.ShapeDtypeStruct((LAYERS, 256, D), F32),
]


def layer_specs(layer):
    return [pl.BlockSpec((1,) + a.shape[1:], lambda i: (layer, 0, 0)) for a in UNPACKED]


def unpack_early(place, near, far):
    return pl.pallas_call(
        put_layer,
        grid=(1,),
        in_specs=[SMEM, VMEM, VMEM],
        out_specs=layer_specs(1),
        out_shape=UNPACKED,
        compiler_params=params(),
        name="unpack_early",
    )(place, near, far)


def unpack_late(place, near, far, *filled):
    return pl.pallas_call(
        unpack_late_kernel,
        grid=(1,),
        in_specs=[SMEM, VMEM, VMEM] + [pl.BlockSpec(memory_space=pl.ANY)] * 3,
        out_specs=layer_specs(0) + [VMEM],
        out_shape=UNPACKED + [jax.ShapeDtypeStruct((LAYERS, 64, D), F32)],
        input_output_aliases={3: 0, 4: 1, 5: 2},
        compiler_params=params(),
        name="unpack_late",
    )(place, near, far, *filled)


def join_kernel(near_ref, far_ref, own_ref, *sent_refs):
    for k in range(4):
        rows = slice(k * TOK, (k + 1) * TOK)
        both = near_ref[rows].astype(F32) + far_ref[rows].astype(F32)
        if k == 0:
            own_ref[...] = both
        else:
            sent_refs[k - 1][...] = both.astype(BF)


def join(near, far):
    sent = jax.ShapeDtypeStruct((TOK, D), BF)
    return pl.pallas_call(
        join_kernel,
        in_specs=[VMEM, VMEM],
        out_specs=[VMEM] * 4,
        out_shape=[jax.ShapeDtypeStruct((TOK, D), F32), sent, sent, sent],
        compiler_params=params(),
        name="join",
    )(near, far)


def rotary_table():
    angle = np.arange(TOK, dtype=np.float64)[:, None] * (10000.0 ** (-2.0 * np.arange(8) / ROT))[None, :]
    lane = np.arange(128) % HEAD_DIM
    cos_n = np.where(lane[None, :] < ROT, np.cos(angle)[:, lane % 8], 1.0)
    low_n = np.where(lane[None, :] < 8, -np.sin(angle)[:, lane % 8], 0.0)
    high_n = np.where((lane[None, :] >= 8) & (lane[None, :] < ROT), np.sin(angle)[:, lane % 8], 0.0)
    rest = np.concatenate([cos_n, low_n, high_n], axis=1).astype(np.float32)
    parts = []
    for _ in range(3):
        parts.append(rest.astype(BF))
        rest = rest - parts[-1].astype(np.float32)
    return np.stack(parts)


def tables_kernel(table_ref, *refs):
    pieces, (mask_ref, cos_ref, low_ref, high_ref) = refs[:REPS], refs[REPS:]
    row = lax.broadcasted_iota(jnp.int32, (TOK, TOK), 0)
    col = lax.broadcasted_iota(jnp.int32, (TOK, TOK), 1)
    for block in range(REPS):
        rows = slice(block * TOK, (block + 1) * TOK)
        docs = jnp.broadcast_to(pieces[block][...].astype(F32)[0:1], (TOK, TOK))
        mask = jnp.where((docs == docs.T) & (col <= row), 1.0, 0.0)
        mask_ref[rows] = mask
        places = jnp.sum(mask, axis=1, keepdims=True) - 1.0
        chosen = jnp.where(col.astype(F32) == places, 1.0, 0.0).astype(BF)
        found = dot(chosen, table_ref[0]) + dot(chosen, table_ref[1]) + dot(chosen, table_ref[2])
        cos_ref[rows] = found[:, :128]
        low_ref[rows] = found[:, 128:256]
        high_ref[rows] = found[:, 256:]


def token_tables(opened):
    return pl.pallas_call(
        tables_kernel,
        grid=(1,),
        in_specs=[VMEM] + [pl.BlockSpec((16, 128), lambda i: (16, 0))] * REPS,
        out_specs=[VMEM] * 4,
        out_shape=[jax.ShapeDtypeStruct((ROWS, 128), F32)] * 4,
        compiler_params=params(),
        name="tables",
    )(jnp.asarray(rotary_table()), *opened)


def turn(values, cos_t, low_t, high_t):
    return values * cos_t + pltpu.roll(values, 120, 1) * low_t + pltpu.roll(values, 8, 1) * high_t


def turn_back(values, cos_t, low_t, high_t):
    return values * cos_t - pltpu.roll(values, 120, 1) * low_t - pltpu.roll(values, 8, 1) * high_t


def row_spec(lanes):
    return pl.BlockSpec((STEP, lanes), lambda i: (i, 0))


def whole_spec(shape):
    return pl.BlockSpec(shape, lambda i: (0,) * len(shape))


PROB_SPEC = pl.BlockSpec((STEP // TOK, 2, TOK, TOK), lambda i: (i, 0, 0, 0))
WA_SPEC = whole_spec((SHARDS, 64, D))
HELD = [pltpu.VMEM((FF_R, D), BF), pltpu.VMEM((128, D), BF)]


def wb_specs(at):
    return [pl.BlockSpec((SHARDS, 16, D), lambda i, k=k: (0, at + k, 0)) for k in range(3)]


def hold_weights(wb_refs, wd_ref, wo_ref):
    @pl.when(pl.program_id(0) == 0)
    def _():
        rows = jnp.concatenate([wb_refs[0][...], wb_refs[1][...]], axis=1)
        wd_ref[...] = rows.reshape(FF_R, D)
        wo_ref[...] = wb_refs[2][...].astype(F32)[:, :8].reshape(128, D).astype(BF)


VEC_SPEC = whole_spec((16, D))
NEAR_SPEC = pl.BlockSpec((STEP, D), lambda i: (jnp.minimum(i, 1), 0))
FAR_SPEC = pl.BlockSpec((STEP, D), lambda i: (jnp.maximum(i - 2, 0), 0))


def rows_of(lanes, dtype):
    return jax.ShapeDtypeStruct((ROWS, lanes), dtype)


def put_block(near_ref, far_ref, values):
    @pl.when(pl.program_id(0) < 2)
    def _():
        near_ref[...] = values

    @pl.when(pl.program_id(0) >= 2)
    def _():
        far_ref[...] = values


def inner_kernel(*refs):
    pieces, (wa_ref, mask_ref, cos_ref, low_ref, high_ref) = refs[:REPS], refs[REPS : REPS + 5]
    xh_ref, qkv_ref, prob_ref, o_ref, act_ref, slope_ref, vec_ref = refs[REPS + 5 :]

    @pl.when(pl.program_id(0) == 0)
    def _():
        side = jnp.zeros((64, 128), F32)
        for shard in range(SHARDS):
            side = side + wa_ref[shard, :, A_LANES:].astype(F32)
        vec_ref[...] = jnp.zeros_like(vec_ref)
        for vector in range(6):
            for j in range(8):
                vec_ref[vector : vector + 1, 128 * j : 128 * (j + 1)] = side[8 * vector + j : 8 * vector + j + 1]
        for j in range(7):
            vec_ref[6:7, 128 * j : 128 * (j + 1)] = side[48 + j : 49 + j]

    for step in range(4):

        @pl.when(pl.program_id(0) == step)
        def _(step=step):
            xh_ref[:TOK] = pieces[2 * step][...]
            xh_ref[TOK:] = pieces[2 * step + 1][...]

    xh = xh_ref[...].astype(F32)
    h1 = (xh * vec_ref[0:1] + vec_ref[1:2]).astype(BF)
    h2 = (xh * vec_ref[2:3] + vec_ref[3:4]).astype(BF)
    mixed = dot(h1, wa_ref[:, :, :QKV_R].reshape(D, QKV_R)) + vec_ref[6:7, :QKV_R]
    tables = (cos_ref[...], low_ref[...], high_ref[...])
    q = turn(mixed[:, :128], *tables).astype(BF)
    k = turn(mixed[:, 128:256], *tables).astype(BF)
    v = mixed[:, 256:].astype(BF)
    qkv_ref[:, :128] = q
    qkv_ref[:, 128:256] = k
    qkv_ref[:, 256:] = v
    u = dot(h2, wa_ref[:, :, QKV_R:A_LANES].reshape(D, FF_R)) + vec_ref[6:7, QKV_R:A_LANES]
    share = 0.5 * (1.0 + lax.erf(u * math.sqrt(0.5)))
    act_ref[...] = (u * share).astype(BF)
    slope_ref[...] = share + u * jnp.exp(-0.5 * u * u) * (1.0 / math.sqrt(2.0 * math.pi))
    first = lax.broadcasted_iota(jnp.int32, (TOK, 128), 1) < HEAD_DIM
    zero = jnp.zeros((TOK, 128), BF)
    for block in range(STEP // TOK):
        rows = slice(block * TOK, (block + 1) * TOK)
        allowed = mask_ref[rows] > 0.5
        out = jnp.zeros((TOK, 128), F32)
        for head in range(2):
            mine = first if head == 0 else jnp.logical_not(first)
            scores = dot_nt(jnp.where(mine, q[rows], zero), k[rows]) * HEAD_DIM**-0.5
            scores = jnp.where(allowed, scores, -1e30)
            raised = jnp.exp(scores - jnp.max(scores, axis=-1, keepdims=True))
            prob = raised / jnp.sum(raised, axis=-1, keepdims=True)
            prob_ref[block, head] = prob
            out = out + dot(prob.astype(BF), jnp.where(mine, v[rows], zero))
        o_ref[rows] = out.astype(BF)


def inner(blocks, wa, masks):
    return pl.pallas_call(
        inner_kernel,
        grid=(ROWS // STEP,),
        in_specs=[whole_spec((TOK, D))] * REPS + [WA_SPEC] + [row_spec(128)] * 4,
        out_specs=[row_spec(D), row_spec(QKV_R), PROB_SPEC, row_spec(128), row_spec(FF_R), row_spec(FF_R), VEC_SPEC],
        out_shape=[
            rows_of(D, BF),
            rows_of(QKV_R, BF),
            jax.ShapeDtypeStruct((REPS, 2, TOK, TOK), F32),
            rows_of(128, BF),
            rows_of(FF_R, BF),
            rows_of(FF_R, F32),
            jax.ShapeDtypeStruct((16, D), F32),
        ],
        compiler_params=params(LARGE),
        name="inner",
    )(*blocks, wa, *masks)


HALF = jax.ShapeDtypeStruct((ROWS // 2, D), BF)


def outer_kernel(o_ref, act_ref, down0_ref, down1_ref, dense_ref, near_ref, far_ref, wd_ref, wo_ref):
    hold_weights((down0_ref, down1_ref, dense_ref), wd_ref, wo_ref)
    part = dot(o_ref[...], wo_ref[...]) + dot(act_ref[...], wd_ref[...])
    put_block(near_ref, far_ref, part.astype(BF))


def outer(attended, act, wb, at):
    return pl.pallas_call(
        outer_kernel,
        grid=(ROWS // STEP,),
        in_specs=[row_spec(128), row_spec(FF_R)] + wb_specs(at),
        out_specs=[NEAR_SPEC, FAR_SPEC],
        out_shape=[HALF, HALF],
        scratch_shapes=HELD,
        compiler_params=params(),
        name="outer",
    )(attended, act, wb, wb, wb)


def backward_kernel(
    e_ref, xh_ref, qkv_ref, prob_ref, slope_ref, wa_ref, down0_ref, down1_ref, dense_ref, vec_ref, cos_ref, low_ref, high_ref,
    near_ref, far_ref, dc_ref, du_ref, side_ref, wd_ref, wo_ref,
):
    def add_row(at, values):
        for j in range(values.shape[1] // 128):
            side_ref[at + j : at + j + 1] += values[:, 128 * j : 128 * (j + 1)]

    @pl.when(pl.program_id(0) == 0)
    def _():
        side_ref[...] = jnp.zeros_like(side_ref)

    hold_weights((down0_ref, down1_ref, dense_ref), wd_ref, wo_ref)
    e = e_ref[...]
    add_row(32, jnp.sum(e.astype(F32), axis=0, keepdims=True))
    du = (dot_nt(e, wd_ref[...]) * slope_ref[...]).astype(BF)
    du_ref[...] = du
    grad_o = dot_nt(e, wo_ref[...]).astype(BF)
    tables = (cos_ref[...], low_ref[...], high_ref[...])
    first = lax.broadcasted_iota(jnp.int32, (TOK, 128), 1) < HEAD_DIM
    zero = jnp.zeros((TOK, 128), BF)
    grads = ([], [], [])
    for block in range(STEP // TOK):
        rows = slice(block * TOK, (block + 1) * TOK)
        q, k, v = qkv_ref[rows, :128], qkv_ref[rows, 128:256], qkv_ref[rows, 256:]
        dq = jnp.zeros((TOK, 128), F32)
        dk = jnp.zeros((TOK, 128), F32)
        dv = jnp.zeros((TOK, 128), F32)
        for head in range(2):
            mine = first if head == 0 else jnp.logical_not(first)
            prob = prob_ref[block, head]
            grad_head = jnp.where(mine, grad_o[rows], zero)
            dv = dv + dot_tn(prob.astype(BF), grad_head)
            grad_prob = dot_nt(grad_head, v)
            inner_sum = jnp.sum(prob * grad_prob, axis=-1, keepdims=True)
            ds = (prob * (grad_prob - inner_sum)).astype(BF)
            dq = dq + dot(ds, jnp.where(mine, k, zero))
            dk = dk + dot_tn(ds, jnp.where(mine, q, zero))
        grads[0].append(dq * HEAD_DIM**-0.5)
        grads[1].append(dk * HEAD_DIM**-0.5)
        grads[2].append(dv)
    dq, dk, dv = (jnp.concatenate(g, axis=0) for g in grads)
    dc = jnp.concatenate([turn_back(dq, *tables), turn_back(dk, *tables), dv], axis=1).astype(BF)
    dc_ref[...] = dc
    dh1 = dot_nt(dc, wa_ref[:, :, :QKV_R].reshape(D, QKV_R))
    dh2 = dot_nt(du, wa_ref[:, :, QKV_R:A_LANES].reshape(D, FF_R))
    put_block(near_ref, far_ref, (dh1 * vec_ref[0:1] + dh2 * vec_ref[2:3]).astype(BF))
    xh = xh_ref[...].astype(F32)
    add_row(0, jnp.sum(dh1 * xh, axis=0, keepdims=True))
    add_row(8, jnp.sum(dh1, axis=0, keepdims=True))
    add_row(16, jnp.sum(dh2 * xh, axis=0, keepdims=True))
    add_row(24, jnp.sum(dh2, axis=0, keepdims=True))
    add_row(40, jnp.sum(dc.astype(F32), axis=0, keepdims=True))
    add_row(43, jnp.sum(du.astype(F32), axis=0, keepdims=True))


def backward(e, kept, wa, wb, at, masks):
    xh, qkv, prob, _, _, slope, vectors = kept
    return pl.pallas_call(
        backward_kernel,
        grid=(ROWS // STEP,),
        in_specs=[row_spec(D), row_spec(D), row_spec(QKV_R), PROB_SPEC, row_spec(FF_R)]
        + [WA_SPEC]
        + wb_specs(at)
        + [VEC_SPEC]
        + [row_spec(128)] * 3,
        out_specs=[NEAR_SPEC, FAR_SPEC, row_spec(QKV_R), row_spec(FF_R), whole_spec((64, 128))],
        out_shape=[
            HALF,
            HALF,
            rows_of(QKV_R, BF),
            rows_of(FF_R, BF),
            jax.ShapeDtypeStruct((64, 128), F32),
        ],
        scratch_shapes=HELD,
        compiler_params=params(LARGE),
        name="backward",
    )(e, xh, qkv, prob, slope, wa, wb, wb, wb, vectors, *masks[1:])


def grad_in_kernel(xh_ref, vec_ref, dc_ref, du_ref, side_ref, out_ref):
    xh = xh_ref[...].astype(F32)
    h1 = (xh * vec_ref[0:1] + vec_ref[1:2]).astype(BF)
    h2 = (xh * vec_ref[2:3] + vec_ref[3:4]).astype(BF)
    out_ref[:, :, :QKV_R] = dot_tn(h1, dc_ref[...]).astype(BF).reshape(4, 64, QKV_R)
    out_ref[:, :, QKV_R:A_LANES] = dot_tn(h2, du_ref[...]).astype(BF).reshape(4, 64, FF_R)
    out_ref[:, :, A_LANES:] = jnp.broadcast_to(side_ref[...].astype(BF)[None], (4, 64, 128))


def grad_all_kernel(xh_ref, vec_ref, dc_ref, du_ref, side_ref, shares_ref, out_ref):
    grad_in_kernel(xh_ref, vec_ref, dc_ref, du_ref, side_ref, out_ref.at[:, :64])
    out_ref[:, 64:] = shares_ref[...]


def grad_all(xh, vectors, dc, du, side, shares):
    return pl.pallas_call(
        grad_all_kernel,
        grid=(4,),
        in_specs=[
            pl.BlockSpec((ROWS, 256), lambda i: (0, i)),
            pl.BlockSpec((16, 256), lambda i: (0, i)),
            whole_spec((ROWS, QKV_R)),
            whole_spec((ROWS, FF_R)),
            whole_spec((64, 128)),
            pl.BlockSpec((4, 48, D), lambda i: (i, 0, 0)),
        ],
        out_specs=pl.BlockSpec((4, 112, D), lambda i: (i, 0, 0)),
        out_shape=jax.ShapeDtypeStruct((SHARDS, 112, D), BF),
        compiler_params=params(),
        name="grad_all",
    )(xh, vectors, dc, du, side, shares)


def grad_in(xh, vectors, dc, du, side):
    return pl.pallas_call(
        grad_in_kernel,
        grid=(4,),
        in_specs=[
            pl.BlockSpec((ROWS, 256), lambda i: (0, i)),
            pl.BlockSpec((16, 256), lambda i: (0, i)),
            whole_spec((ROWS, QKV_R)),
            whole_spec((ROWS, FF_R)),
            whole_spec((64, 128)),
        ],
        out_specs=pl.BlockSpec((4, 64, D), lambda i: (i, 0, 0)),
        out_shape=jax.ShapeDtypeStruct((SHARDS, 64, D), BF),
        compiler_params=params(),
        name="grad_in",
    )(xh, vectors, dc, du, side)


def grad_out_kernel(o_ref, act_ref, *refs):
    pieces, (out_ref, e_ref) = refs[:REPS], refs[REPS:]
    e = jnp.concatenate([piece[...] for piece in pieces], axis=0)
    e_ref[...] = e
    down = dot_tn(act_ref[...], e).reshape(SHARDS, UNIT, 256)
    dense = dot_tn(o_ref[...], e).reshape(SHARDS, 8, 256)
    empty = jnp.zeros((SHARDS, 8, 256), F32)
    out_ref[...] = jnp.concatenate([down, dense, empty], axis=1).astype(BF)


def grad_out_of(attended, act, blocks, at):
    return pl.pallas_call(
        grad_out_kernel,
        grid=(4,),
        in_specs=[
            whole_spec((ROWS, 128)),
            whole_spec((ROWS, FF_R)),
        ]
        + [pl.BlockSpec((TOK, 256), lambda i: (at, i))] * REPS,
        out_specs=[
            pl.BlockSpec((SHARDS, 48, 256), lambda i: (0, 0, i)),
            pl.BlockSpec((ROWS, 256), lambda i: (0, i)),
        ],
        out_shape=[jax.ShapeDtypeStruct((SHARDS, 48, D), BF), rows_of(D, BF)],
        compiler_params=params(),
        name="grad_out",
    )(attended, act, *blocks)


def standardize(x):
    centered = x - jnp.mean(x, axis=-1, keepdims=True)
    scale = lax.rsqrt(jnp.mean(centered * centered, axis=-1, keepdims=True) + EPS)
    return centered * scale, scale


def in_order(near, far, c):
    return jnp.stack([jnp.where(c == 0, near, far), jnp.where(c == 0, far, near)], axis=1).reshape((REPS,) + near.shape[1:])


def per_device(
    tokens, doc_ids, grad_out, norm_gains, shifts, qkv_weight, qkv_bias, dense_weight, up_weight, up_bias, down_weight
):
    r = lax.axis_index("rep").astype(jnp.int32)
    s = lax.axis_index("shard").astype(jnp.int32)
    y, c = r // 2, r % 2
    place = jnp.stack([r, s])

    dense = lax.dynamic_slice_in_dim(dense_weight, 8 * r, 8, 1)
    dense = lax.ppermute(dense, ("rep", "shard"), DENSE_IN)
    first, late, packed_b = pack(place, qkv_weight, up_weight, down_weight, norm_gains, shifts, qkv_bias, up_bias)
    packed_b = jnp.concatenate([packed_b, dense, jnp.zeros((LAYERS, 8, D), BF)], axis=1)
    wa0 = exchange_shard(first)
    wb0 = lax.all_gather(packed_b[0], "shard", axis=0)

    current = tokens.astype(F32)
    hat, scale = standardize(current)
    live = (doc_ids >= 0).astype(F32)[:, None]
    grad_y = grad_out.astype(F32) * live
    marks = jnp.pad(doc_ids.astype(BF).reshape(1, TOK), ((0, 15), (0, D - TOK)))
    opened = gather_rep(jnp.concatenate([hat.astype(BF), grad_y.astype(BF), marks], axis=0))
    masks = token_tables(opened)

    late = jnp.concatenate([late, packed_b[1]], axis=0)
    late, wa0, opened = lax.optimization_barrier((late, wa0, opened))
    late = lax.all_gather(late, "shard", axis=0)

    saved0 = inner(opened, wa0, masks)
    own, moved = scatter_rep(*outer(saved0[3], saved0[4], wb0, 0))
    hat0, scale0 = hat, scale
    current = current + total_of(own, moved) + saved0[6][4:5] + saved0[6][5:6]
    hat, scale = standardize(current)
    saved1 = inner(gather_rep(hat.astype(BF)), late, masks)

    def input_grad_of(dy, hat, scale, total):
        shared = jnp.mean(total, axis=-1, keepdims=True)
        along = jnp.mean(total * hat, axis=-1, keepdims=True)
        return dy + scale * (total - shared - hat * along)

    shares, e = grad_out_of(saved1[3], saved1[4], opened, 1)
    raw_b1 = exchange_shard(shares)
    near, far, *grads = backward(e, saved1, late, late, 4, masks)
    own, moved = scatter_rep(near, far)
    grad_y = input_grad_of(grad_y, hat, scale, total_of(own, moved))
    blocks = gather_rep(grad_y.astype(BF))
    grads, _ = lax.optimization_barrier((grads, blocks[1]))
    raw_a1 = exchange_shard(grad_in(saved1[0], saved1[6], *grads))
    attended, act, _ = lax.optimization_barrier((saved1[3], saved1[4], blocks[1]))
    part = outer(attended, act, late, 4)

    shares, e = grad_out_of(saved0[3], saved0[4], blocks, 0)
    near, far, *grads = backward(e, saved0, wa0, wb0, 0, masks)
    raw0 = exchange_shard(grad_all(saved0[0], saved0[6], *grads, shares))
    part, near, raw_a1, raw_b1, _ = lax.optimization_barrier((part, near, raw_a1, raw_b1, grads))
    in_own, in_moved = scatter_rep(near, far)
    out_own, out_moved = scatter_rep(*part)
    sum_a1, sum_b1 = add_up(raw_a1), add_up(raw_b1)
    early = jnp.concatenate([sum_a1, sum_b1[:UNIT]], axis=0)
    early = in_y_order([early] + [fetch_y(early, k) for k in (1, 2, 3)], y)
    early = (early, flip_core(early))
    grad_qkv, grad_up, grad_down = unpack_early(place, *early)
    raw0, out_moved, in_moved = lax.optimization_barrier((raw0, out_moved, in_moved))
    sum0 = add_up(raw0)
    grad_y = input_grad_of(grad_y, hat0, scale0, total_of(in_own, in_moved))
    output = (current + total_of(out_own, out_moved) + saved1[6][4:5] + saved1[6][5:6]).astype(BF)
    moved = jnp.concatenate([sum_b1[UNIT:], sum0[64 + UNIT :]], axis=0)
    moved = lax.ppermute(moved, ("rep", "shard"), DENSE_OUT)
    ending = jnp.concatenate([sum0[: 64 + UNIT], moved], axis=0)
    ending = along_y(jnp.broadcast_to(ending[None], (4, TOK, D)))
    held = lax.optimization_barrier((ending, grad_qkv, grad_up, grad_down, grad_y, output))
    ending, grad_qkv, grad_up, grad_down, grad_y, output = held
    ending = (ending, flip_core(ending))
    grad_qkv, grad_up, grad_down, grad_dense = unpack_late(place, *ending, grad_qkv, grad_up, grad_down)

    pieces = (ending, early)
    sides = [in_order(p[0][:, :47, A_LANES:], p[1][:, :47, A_LANES:], c).astype(F32) for p in pieces]
    side = jnp.stack(sides)
    sums = jnp.sum(side[:, :, :32], axis=1)
    sums = jnp.concatenate([sums, side[:, 0, 32:40]], axis=1).reshape(LAYERS, 5, D)
    sums = lax.dynamic_slice_in_dim(sums, 64 * s, 64, 2)
    grad_gains = jnp.stack([sums[:, 0], sums[:, 2]], axis=1)
    grad_shifts = jnp.stack([sums[:, 1], sums[:, 3], sums[:, 4], sums[:, 4]], axis=1)
    qkv_b = jnp.swapaxes(side[:, :, 40:43], 1, 2).reshape(LAYERS, 3 * D)
    grad_qkv_bias = lax.dynamic_slice_in_dim(qkv_b, 192 * s, 192, 1)
    up_b = side[:, :, 43:].reshape(LAYERS, REPS, FF_R)
    grad_up_bias = lax.dynamic_slice_in_dim(up_b, UNIT * s, UNIT, 2).reshape(LAYERS, 256)
    return (
        output,
        grad_y,
        grad_gains,
        grad_shifts,
        grad_qkv,
        grad_qkv_bias,
        grad_dense,
        grad_up,
        grad_up_bias,
        grad_down,
    )


def solution(mesh):
    return jax.shard_map(
        per_device,
        mesh=mesh,
        in_specs=(
            P(("rep", "shard"), None),
            P(("rep", "shard")),
            P(("rep", "shard"), None),
            P(None, None, "shard"),
            P(None, None, "shard"),
            P(None, "shard", None),
            P(None, "shard"),
            P(None, "shard", None),
            P(None, "shard", None),
            P(None, "shard"),
            P(None, "shard", None),
        ),
        out_specs=(
            P(("rep", "shard"), None),
            P(("rep", "shard"), None),
            P(None, None, "shard"),
            P(None, None, "shard"),
            P(None, "shard", None),
            P(None, "shard"),
            P(None, "shard", None),
            P(None, "shard", None),
            P(None, "shard"),
            P(None, "shard", None),
        ),
        check_vma=False,
    )
```
